128 devices in a mesh: grp: 4 (over y), fac: 32 (over z, x, core).
Axes of the slice: x: 4, y: 4, z: 4, core: 2. Of those that a mesh axis runs over, the one named last changes fastest.
Arguments:
- image_cube: float32 [32, 6144, 256], P('fac', 'grp'), may hold values from -6 to 6
- dual: bfloat16 [8, 32, 9216, 256], P(None, None, ('grp', 'fac')), may hold values from -6 to 6
- lowpass: bfloat16 [2, 4], replicated, may hold values from -2.5 to 2.5, as said below
- thresholds: float32 [8], replicated, may hold values from 4 to 16
- facet_rows: int32 [4, 32], replicated, may hold values from 24 to 72, as said below
Outputs:
- dual_next: bfloat16 [8, 32, 9216, 256], P(None, None, ('grp', 'fac'))
- prior_term: float32 [32, 6144, 256], P('fac', 'grp')
The draws below stay inside these ranges and needn't reach their ends.
Inputs may be any that keep to these rules, and one draw needn't show every extreme that they name: `facet_rows`: every row sums to 1536; in every row some facet has exactly 72 rows and some exactly 24. `lowpass`: row d has nonzero taps only at positions 2 - d - 1 to 2 + d.
All inputs are finite; a program needn't handle non-finite values.
Results may differ from the reference program's by a relative error of at most 0.0035.
Values sent between devices are 32-bit elements; how exact they have to be, the bound alone decides.
No kernel may reach another device: no remote copies, remote signals or barrier semaphores. Data moves between devices by JAX's collectives and lax.ppermute only.
A program may use at most 128 MiB of HBM per device.

```python
import math
import jax
import jax.numpy as jnp
from jax import lax

C = 32
NDICT = 2
RMEAN = 48
W = 256
RCAP = 72
BANDS = 4
FACETS = 32
NROWS = 6144
SLOTS = 9216
NSUB = 8


def draw_lowpass(key, part):
    tap_positions = jnp.arange(2 * NDICT)
    half_widths = jnp.arange(NDICT) + 1
    support = (tap_positions[None, :] >= NDICT - half_widths[:, None]) & (tap_positions[None, :] < NDICT + half_widths[:, None])
    samples = jnp.clip(jax.random.normal(key, (NDICT, 2 * NDICT), jnp.float32), -3.5, 3.5)
    scaled = jnp.where(support, samples, 0.0) / jnp.sqrt(2.0 * half_widths.astype(jnp.float32))[:, None]
    return scaled.astype(jnp.bfloat16)


def draw_facet_rows(key, part):
    first_key = jax.random.fold_in(key, 11)
    second_key = jax.random.fold_in(key, 23)
    spread_rows = RMEAN // 2
    pairs = FACETS // 2
    shifts_drawn = jax.random.randint(first_key, (BANDS, pairs), -spread_rows, spread_rows + 1)
    forced_pair = jax.random.randint(second_key, (BANDS, 1), 0, pairs)
    shifts_drawn = jnp.where(jnp.arange(pairs)[None, :] == forced_pair, spread_rows, shifts_drawn)
    lengths = jnp.stack([RMEAN + shifts_drawn, RMEAN - shifts_drawn], axis=-1).reshape(BANDS, FACETS)
    return lengths.astype(jnp.int32)


def level_of(rng, dims, cuts, low, largest):
    def one(dim, blocks):
        steps = jax.random.uniform(jax.random.fold_in(jax.random.fold_in(rng, 6), dim), (blocks,), jnp.float32, low / len(cuts), largest / len(cuts))
        return jnp.repeat(jnp.exp(steps), dims[dim] // blocks).reshape((-1,) + (1,) * (len(dims) - dim - 1))

    level = one(*cuts[0])
    for cut in cuts[1:]:
        level = level * one(*cut)
    return level


def gaussian(rng, dims, width, bound, shards=(), kind=jnp.bfloat16):
    gain = level_of(rng, dims, shards, -0.22, 0.18) if shards else 1.0
    result = jax.random.normal(rng, dims, jnp.float32) * width * gain
    return jnp.minimum(jnp.maximum(result, -bound), bound).astype(kind)


def setup_inputs(seed: int = 0) -> dict:
    arg_keys = jax.random.split(jax.random.key(seed), 6)
    return {
        "image_cube": gaussian(arg_keys[0], (C, NROWS, W), 1.0, 6.0, ((0, 32), (1, 4)), jnp.float32),
        "dual": gaussian(arg_keys[1], (NSUB, C, SLOTS, W), 1.0, 6.0, ((2, 128),)),
        "lowpass": draw_lowpass(jax.random.fold_in(arg_keys[5], 71), 0),
        "thresholds": jnp.clip(jnp.exp(jax.random.uniform(arg_keys[3], (NSUB,), jnp.float32, math.log(4.0), math.log(16.0))), 4.0, 16.0),
        "facet_rows": draw_facet_rows(jax.random.fold_in(arg_keys[5], 71), 0),
    }


def highpass(lowpass_row):
    tap_count = lowpass_row.shape[0]
    parity = jnp.where(jnp.arange(tap_count) % 2 == 0, 1.0, -1.0).astype(jnp.float32)
    return parity * lowpass_row[::-1]

def forward_conv(source, filter_taps, along):
    halo_rows = filter_taps.shape[0] // 2
    length = source.shape[along]
    widths = [(0, 0)] * source.ndim
    widths[along] = (halo_rows, halo_rows)
    padded = jnp.pad(source, widths)
    summed = jnp.zeros_like(source)
    for offset in range(2 * halo_rows):
        summed = summed + filter_taps[offset] * lax.slice_in_dim(padded, offset, offset + length, axis=along)
    return summed

def adjoint_conv(source, filter_taps, along):
    halo_rows = filter_taps.shape[0] // 2
    length = source.shape[along]
    widths = [(0, 0)] * source.ndim
    widths[along] = (halo_rows, halo_rows)
    padded = jnp.pad(source, widths)
    summed = jnp.zeros_like(source)
    for offset in range(2 * halo_rows):
        begin = 2 * halo_rows - offset
        summed = summed + filter_taps[offset] * lax.slice_in_dim(padded, begin, begin + length, axis=along)
    return summed

def reference(image_cube, dual, lowpass, thresholds, facet_rows):
    filters_wide = lowpass.astype(jnp.float32)
    lengths = facet_rows.reshape(-1).astype(jnp.int32)
    starts = jnp.cumsum(lengths) - lengths
    positions = jnp.arange(RCAP, dtype=jnp.int32)
    slot_rows = (starts[:, None] + positions[None, :]).reshape(-1)
    slot_rows = jnp.clip(slot_rows, 0, NROWS - 1).astype(jnp.int32)
    slot_valid = (positions[None, :] < lengths[:, None]).reshape(-1)
    slot_mask = slot_valid.astype(jnp.float32)[None, :, None]
    row_numbers = jnp.arange(NROWS, dtype=jnp.int32)
    owner_facet = lax.optimization_barrier(jnp.sum((starts[None, :] <= row_numbers[:, None]).astype(jnp.int32), axis=1)) - 1
    row_slots = (owner_facet * RCAP + row_numbers - starts[owner_facet]).astype(jnp.int32)
    prior_term = jnp.zeros((C, NROWS, W), jnp.float32)
    updated = []
    for dict_index in range(NDICT):
        low_taps = filters_wide[dict_index]
        filter_pair = [low_taps, highpass(low_taps)]
        filtered = [forward_conv(image_cube, filter_pair[kind], 2) for kind in range(2)]
        row_sums = [jnp.zeros((C, NROWS, W), jnp.float32), jnp.zeros((C, NROWS, W), jnp.float32)]
        for row_kind in range(2):
            for column_kind in range(2):
                subband = 4 * dict_index + 2 * row_kind + column_kind
                coefficient = forward_conv(filtered[column_kind], filter_pair[row_kind], 1)
                combined = (dual[subband].astype(jnp.float32) + coefficient[:, slot_rows, :]) * slot_mask
                magnitude = jnp.sqrt(lax.optimization_barrier(jnp.sum(combined * combined, axis=0)))
                radius = thresholds[subband]
                scaled = (combined * (radius / jnp.maximum(magnitude, radius))).astype(jnp.bfloat16)
                updated.append(scaled)
                restored = scaled[:, row_slots, :].astype(jnp.float32)
                row_sums[column_kind] = row_sums[column_kind] + adjoint_conv(restored, filter_pair[row_kind], 1)
        for column_kind in range(2):
            prior_term = prior_term + adjoint_conv(row_sums[column_kind], filter_pair[column_kind], 2)
    return (jnp.stack(updated, 0), prior_term)
```

```python
import functools

import jax
import jax.numpy as jnp
from jax import lax
from jax.experimental import pallas as pl
from jax.experimental.pallas import tpu as pltpu
from jax.sharding import PartitionSpec as P

TAPS = 4
ABOVE = 2
MARGIN = 8
LANES = 128


def shifted(x, axis, by):
    devices = lax.axis_size(axis)
    pairs = [(i, i + by) for i in range(devices) if 0 <= i + by < devices]
    return lax.ppermute(x, axis, pairs)


def filter_taps(lowpass):
    low = lowpass.astype(jnp.float32)
    parity = jnp.where(jnp.arange(TAPS) % 2 == 0, 1.0, -1.0).astype(jnp.float32)
    return jnp.stack([low, parity * low[:, ::-1]], axis=1)


def column_matrices(taps, columns):
    row = jnp.arange(columns)[:, None]
    col = jnp.arange(columns)[None, :]
    offset = row - col + 2
    total = 0.0
    for k in range(TAPS):
        hit = (offset == k)[None, None]
        total = total + jnp.where(hit, taps[:, :, k, None, None], 0.0)
    return total.astype(jnp.bfloat16)


def facet_starts(rows_ref, starts_ref, facets):
    def step(q, total):
        starts_ref[q] = total
        return total + rows_ref[q]

    lax.fori_loop(0, facets, step, jnp.int32(0))


def pack_kernel(per_step, ext, rows_ref, image_ref, upper_ref, lower_ref, out_ref, strip, starts, sem):
    step = pl.program_id(0)
    band_rows = image_ref.shape[1]
    facets = rows_ref.shape[0]

    @pl.when(step == 0)
    def _():
        copies = [
            pltpu.make_async_copy(
                image_ref.at[0, :, pl.ds(h * LANES, LANES)],
                strip.at[h, pl.ds(MARGIN, band_rows)],
                sem.at[h],
            )
            for h in range(2)
        ]
        for copy in copies:
            copy.start()
        facet_starts(rows_ref, starts, facets)
        for h in range(2):
            lanes = slice(h * LANES, (h + 1) * LANES)
            strip[h, 0:MARGIN] = jnp.zeros((MARGIN, LANES), jnp.float32)
            strip[h, MARGIN - ABOVE : MARGIN] = upper_ref[0, :, lanes]
            tail = strip.shape[1] - MARGIN - band_rows
            strip[h, MARGIN + band_rows :] = jnp.zeros((tail, LANES), jnp.float32)
            strip[h, MARGIN + band_rows : MARGIN + band_rows + ABOVE] = lower_ref[0, :, lanes]
        for copy in copies:
            copy.wait()

    for q in range(per_step):
        begin = starts[step * per_step + q] + (MARGIN - ABOVE)
        for h in range(2):
            out_ref[q, h * ext : (h + 1) * ext] = strip[h, pl.ds(begin, ext)]


def unpack_kernel(per_step, ext, rows_ref, block_ref, from_next_ref, from_prev_ref, out_ref, strip, starts, sem):
    step = pl.program_id(0)
    band_rows = out_ref.shape[1]
    facets = rows_ref.shape[0]

    @pl.when(step == 0)
    def _():
        facet_starts(rows_ref, starts, facets)
        for h in range(2):
            strip[h, 0 : 2 * MARGIN] = jnp.zeros((2 * MARGIN, LANES), jnp.float32)

    shared = lax.broadcasted_iota(jnp.int32, (8, LANES), 0) < 3
    for q in range(per_step):
        begin = starts[step * per_step + q] + (MARGIN - ABOVE)
        for h in range(2):
            before = strip[h, pl.ds(begin, 8)]
            strip[h, pl.ds(begin, 8)] = block_ref[q, h * ext : h * ext + 8] + jnp.where(shared, before, 0.0)
            strip[h, pl.ds(begin + 8, ext - 8)] = block_ref[q, h * ext + 8 : (h + 1) * ext]

    @pl.when(step == pl.num_programs(0) - 1)
    def _():
        copies = []
        for h in range(2):
            strip[h, MARGIN : MARGIN + 1] += from_prev_ref[h]
            end = MARGIN + band_rows
            strip[h, end - ABOVE : end] += from_next_ref[h]
            copies.append(
                pltpu.make_async_copy(
                    strip.at[h, pl.ds(MARGIN, band_rows)],
                    out_ref.at[0, :, pl.ds(h * LANES, LANES)],
                    sem.at[h],
                )
            )
        for copy in copies:
            copy.start()
        for copy in copies:
            copy.wait()


def facet_kernel(group, ext, taps_ref, thr_ref, len_ref, x_ref, dual_ref, fwd_ref, adj_ref,
                 next_ref, merged_ref, u_ref, sq_ref, z_ref):
    step = pl.program_id(0)
    channels, capacity, columns = dual_ref.shape[1:]
    dict_index = step // 2
    taps = [taps_ref[step * TAPS + k] for k in range(TAPS)]
    rows = group * capacity

    @pl.when(step == 0)
    def _():
        merged_ref[...] = jnp.zeros_like(merged_ref)
        z_ref[...] = jnp.zeros_like(z_ref)

    sq_ref[...] = jnp.zeros_like(sq_ref)

    def analyse(i, carry):
        pick = pl.ds(i * group, group)
        halves = []
        for h in range(2):
            total = taps[0] * x_ref[pick, h * ext : h * ext + capacity, :]
            for k in range(1, TAPS):
                total = total + taps[k] * x_ref[pick, h * ext + k : h * ext + k + capacity, :]
            halves.append(total.reshape(rows, LANES))
        filtered = jnp.concatenate(halves, axis=1)
        high = filtered.astype(jnp.bfloat16)
        low = (filtered - high.astype(jnp.float32)).astype(jnp.bfloat16)
        coefficient = jnp.dot(
            jnp.concatenate([high, low], axis=1), fwd_ref[dict_index], preferred_element_type=jnp.float32
        )
        for b in range(2):
            part = coefficient[:, b * columns : (b + 1) * columns].reshape(group, capacity, columns)
            combined = part + dual_ref[b, pick].astype(jnp.float32)
            u_ref[b, pick] = combined
            sq_ref[b] += jnp.sum(combined * combined, axis=0)
        return carry

    lax.fori_loop(0, channels // group, analyse, 0)

    keep = lax.broadcasted_iota(jnp.int32, (capacity, columns), 0) < len_ref[0]
    for b in range(2):
        radius = thr_ref[step * 2 + b]
        scale = radius / jnp.maximum(jnp.sqrt(sq_ref[b]), radius)
        sq_ref[b] = jnp.where(keep, scale, 0.0)

    def synthesise(i, carry):
        pick = pl.ds(i * group, group)
        parts = []
        for b in range(2):
            scaled = u_ref[b, pick] * sq_ref[b][None]
            next_ref[b, pick] = scaled.astype(jnp.bfloat16)
            parts.append(scaled.reshape(rows, columns).astype(jnp.bfloat16))
        z = jnp.dot(jnp.concatenate(parts, axis=1), adj_ref[dict_index], preferred_element_type=jnp.float32)
        z = z.reshape(group, capacity, columns)
        for h in range(2):
            z_ref[h, :, 8 : 8 + capacity, :] = z[:, :, h * LANES : (h + 1) * LANES]
        for h in range(2):
            total = taps[0] * z_ref[h, :, 8 : 8 + ext, :]
            for k in range(1, TAPS):
                total = total + taps[k] * z_ref[h, :, 8 - k : 8 - k + ext, :]
            merged_ref[pick, h * ext : (h + 1) * ext, :] += total
        return carry

    lax.fori_loop(0, channels // group, synthesise, 0)


def on_device(image_cube, dual, lowpass, thresholds, facet_rows):
    band = lax.axis_index("grp")
    facet = lax.axis_index("fac")
    facets = lax.axis_size("fac")
    _, band_rows, columns = image_cube.shape
    subbands, channels, capacity, _ = dual.shape
    ext = capacity + TAPS
    per_step = 8
    strip_rows = MARGIN + band_rows + capacity
    lengths = lax.dynamic_index_in_dim(facet_rows, band, 0, keepdims=False)
    own_length = lax.dynamic_slice_in_dim(lengths, facet, 1)

    upper = shifted(image_cube[:, -ABOVE:], "grp", 1)
    lower = shifted(image_cube[:, :ABOVE], "grp", -1)
    row_scratch = [
        pltpu.VMEM((2, strip_rows, LANES), jnp.float32),
        pltpu.SMEM((facets,), jnp.int32),
        pltpu.SemaphoreType.DMA((2,)),
    ]
    blocks = pl.BlockSpec((per_step, 2 * ext, LANES), lambda i, *_: (i, 0, 0))
    smem = pl.BlockSpec(memory_space=pltpu.SMEM)
    vmem = pl.BlockSpec(memory_space=pltpu.VMEM)
    hbm = pl.BlockSpec(memory_space=pl.ANY)
    packed = pl.pallas_call(
        functools.partial(pack_kernel, per_step, ext),
        grid=(facets // per_step,),
        out_shape=jax.ShapeDtypeStruct((facets, 2 * ext, LANES), jnp.float32),
        in_specs=[smem, hbm, vmem, vmem],
        out_specs=blocks,
        scratch_shapes=row_scratch,
        compiler_params=pltpu.CompilerParams(vmem_limit_bytes=16 << 20),
        name="pack_facets",
    )(lengths, image_cube, upper, lower)

    received = lax.all_to_all(packed, "fac", split_axis=0, concat_axis=0, tiled=True)

    taps = filter_taps(lowpass)
    matrices = column_matrices(taps, columns)
    forward = jnp.concatenate([matrices[:, 0], matrices[:, 1]], axis=2)
    forward = jnp.concatenate([forward, forward], axis=1)
    swapped = jnp.swapaxes(matrices, 2, 3)
    adjoint = jnp.concatenate([swapped[:, 0], swapped[:, 1]], axis=1)
    group = 4
    steps = subbands // 2
    pair = pl.BlockSpec((2, channels, capacity, columns), lambda i: (i, 0, 0, 0))
    whole = pl.BlockSpec((channels, 2 * ext, LANES), lambda i: (0, 0, 0))
    dual_next, merged = pl.pallas_call(
        functools.partial(facet_kernel, group, ext),
        grid=(steps,),
        out_shape=(
            jax.ShapeDtypeStruct(dual.shape, jnp.bfloat16),
            jax.ShapeDtypeStruct((channels, 2 * ext, LANES), jnp.float32),
        ),
        in_specs=[
            smem, smem, smem, whole, pair,
            pl.BlockSpec(forward.shape, lambda i: (0, 0, 0)),
            pl.BlockSpec(adjoint.shape, lambda i: (0, 0, 0)),
        ],
        out_specs=(pair, whole),
        scratch_shapes=[
            pltpu.VMEM((2, channels, capacity, columns), jnp.float32),
            pltpu.VMEM((2, capacity, columns), jnp.float32),
            pltpu.VMEM((2, group, capacity + 16, LANES), jnp.float32),
        ],
        compiler_params=pltpu.CompilerParams(vmem_limit_bytes=48 << 20),
        name="facet_update",
    )(taps.reshape(-1), thresholds, own_length, received, dual, forward, adjoint)

    returned = lax.all_to_all(merged, "fac", split_axis=0, concat_axis=0, tiled=True)

    first = jnp.stack([returned[0, h * ext : h * ext + ABOVE] for h in range(2)])
    below = capacity * 0 + lengths[facets - 1] + ABOVE
    last = jnp.stack(
        [lax.dynamic_slice_in_dim(returned[facets - 1, h * ext : (h + 1) * ext], below, 1) for h in range(2)]
    )
    from_next = shifted(first, "grp", -1)
    from_prev = shifted(last, "grp", 1)
    prior_term = pl.pallas_call(
        functools.partial(unpack_kernel, per_step, ext),
        grid=(facets // per_step,),
        out_shape=jax.ShapeDtypeStruct(image_cube.shape, jnp.float32),
        in_specs=[smem, blocks, vmem, vmem],
        out_specs=hbm,
        scratch_shapes=row_scratch,
        compiler_params=pltpu.CompilerParams(vmem_limit_bytes=16 << 20),
        name="unpack_facets",
    )(lengths, returned, from_next, from_prev)
    return dual_next, prior_term


def solution(mesh):
    placed = (P("fac", "grp", None), P(None, None, ("grp", "fac"), None), P(), P(), P())
    return jax.shard_map(
        on_device,
        mesh=mesh,
        in_specs=placed,
        out_specs=(P(None, None, ("grp", "fac"), None), P("fac", "grp", None)),
        check_vma=False,
    )
```

```python
import functools

import jax
import jax.numpy as jnp
from jax import lax
from jax.experimental import pallas as pl
from jax.experimental.pallas import tpu as pltpu
from jax.sharding import PartitionSpec as P

TAPS = 4
ABOVE = 2
MARGIN = 8
LANES = 128


def border_shift(x, bands, facets, by):
    pairs = []
    for b in range(bands):
        for facet in range(facets):
            to = b + by if facet < facets // 2 else b - by
            pairs.append((b * facets + facet, (to % bands) * facets + facet))
    return lax.ppermute(x, ("grp", "fac"), pairs)


def filter_taps(lowpass):
    low = lowpass.astype(jnp.float32)
    parity = jnp.where(jnp.arange(TAPS) % 2 == 0, 1.0, -1.0).astype(jnp.float32)
    return jnp.stack([low, parity * low[:, ::-1]], axis=1)


def column_matrices(taps, columns):
    row = jnp.arange(columns)[:, None]
    col = jnp.arange(columns)[None, :]
    offset = row - col + 2
    total = 0.0
    for k in range(TAPS):
        hit = (offset == k)[None, None]
        total = total + jnp.where(hit, taps[:, :, k, None, None], 0.0)
    return total.astype(jnp.bfloat16)


def facet_starts(rows_ref, starts_ref, facets):
    band = lax.axis_index("grp")

    def step(q, total):
        starts_ref[q] = total
        return total + rows_ref[band, q]

    lax.fori_loop(0, facets, step, jnp.int32(0))


def pack_kernel(per_copy, ext, rows_ref, image_ref, out_ref, strip, starts, blocks, in_sem, out_sem):
    band_rows = image_ref.shape[1]
    facets = rows_ref.shape[1]
    copies = [
        pltpu.make_async_copy(
            image_ref.at[0, :, pl.ds(h * LANES, LANES)], strip.at[h, pl.ds(MARGIN, band_rows)], in_sem.at[h]
        )
        for h in range(2)
    ]
    for copy in copies:
        copy.start()
    facet_starts(rows_ref, starts, facets)
    end = MARGIN + band_rows
    for h in range(2):
        strip[h, 0:MARGIN] = jnp.zeros((MARGIN, LANES), jnp.float32)
        strip[h, end:] = jnp.zeros((strip.shape[1] - end, LANES), jnp.float32)
    for copy in copies:
        copy.wait()
    for h in range(2):
        strip[h, MARGIN - ABOVE : MARGIN] = strip[h, end - ABOVE : end]
        strip[h, end : end + 1] = strip[h, MARGIN : MARGIN + 1]

    outs = []
    for g in range(facets // per_copy):
        for q in range(g * per_copy, (g + 1) * per_copy):
            begin = starts[q] + (MARGIN - ABOVE)
            for h in range(2):
                blocks[q, h * ext : (h + 1) * ext] = strip[h, pl.ds(begin, ext)]
        pick = pl.ds(g * per_copy, per_copy)
        outs.append(pltpu.make_async_copy(blocks.at[pick], out_ref.at[pick], out_sem.at[g]))
        outs[-1].start()
    for copy in outs:
        copy.wait()


def unpack_kernel(per_step, ext, rows_ref, block_ref, out_ref, strip, starts, sem):
    step = pl.program_id(0)
    band_rows = out_ref.shape[1]
    facets = rows_ref.shape[1]

    @pl.when(step == 0)
    def _():
        facet_starts(rows_ref, starts, facets)
        for h in range(2):
            strip[h, 0 : 2 * MARGIN] = jnp.zeros((2 * MARGIN, LANES), jnp.float32)

    shared = lax.broadcasted_iota(jnp.int32, (8, LANES), 0) < 3
    for q in range(per_step):
        begin = starts[step * per_step + q] + (MARGIN - ABOVE)
        for h in range(2):
            before = strip[h, pl.ds(begin, 8)]
            strip[h, pl.ds(begin, 8)] = block_ref[q, h * ext : h * ext + 8] + jnp.where(shared, before, 0.0)
            strip[h, pl.ds(begin + 8, ext - 8)] = block_ref[q, h * ext + 8 : (h + 1) * ext]

    @pl.when(step == pl.num_programs(0) - 1)
    def _():
        copies = []
        end = MARGIN + band_rows
        for h in range(2):
            strip[h, end - ABOVE : end] += strip[h, MARGIN - ABOVE : MARGIN]
            strip[h, MARGIN : MARGIN + 1] += strip[h, end : end + 1]
            copies.append(
                pltpu.make_async_copy(
                    strip.at[h, pl.ds(MARGIN, band_rows)],
                    out_ref.at[0, :, pl.ds(h * LANES, LANES)],
                    sem.at[h],
                )
            )
        for copy in copies:
            copy.start()
        for copy in copies:
            copy.wait()


def facet_kernel(group, ext, taps_ref, thr_ref, info_ref, edge_ref, x_hbm, dual_ref, fwd_ref, adj_ref,
                 next_ref, merged_ref, spill_ref, x_ref, u_ref, sq_ref, z_ref, in_sem):
    step = pl.program_id(0)
    channels, capacity, columns = dual_ref.shape[1:]
    dict_index = step // 2
    taps = [taps_ref[step * TAPS + k] for k in range(TAPS)]
    rows = group * capacity
    length, below, above = info_ref[0], info_ref[1], info_ref[2]
    inside = info_ref[3].astype(jnp.float32)

    def incoming(i):
        pick = pl.ds(i * group, group)
        return pltpu.make_async_copy(x_hbm.at[pick], x_ref.at[pick], in_sem.at[i])

    @pl.when(step == 0)
    def _():
        for i in range(channels // group):
            incoming(i).start()
        merged_ref[...] = jnp.zeros_like(merged_ref)
        z_ref[...] = jnp.zeros_like(z_ref)

    sq_ref[...] = jnp.zeros_like(sq_ref)

    def analyse(i, carry):
        pick = pl.ds(i * group, group)

        @pl.when(step == 0)
        def _():
            incoming(i).wait()

            @pl.when(above == 1)
            def _():
                for h in range(2):
                    x_ref[pick, h * ext : h * ext + ABOVE, :] = inside * edge_ref[pick, ABOVE * h : ABOVE * (h + 1), :]

            @pl.when(below == 1)
            def _():
                for h in range(2):
                    row = pl.ds(h * ext + ABOVE + length, 1)
                    x_ref[pick, row, :] = inside * edge_ref[pick, ABOVE * h : ABOVE * h + 1, :]

        halves = []
        for h in range(2):
            total = taps[0] * x_ref[pick, h * ext : h * ext + capacity, :]
            for k in range(1, TAPS):
                total = total + taps[k] * x_ref[pick, h * ext + k : h * ext + k + capacity, :]
            halves.append(total.reshape(rows, LANES))
        filtered = jnp.concatenate(halves, axis=1)
        high = filtered.astype(jnp.bfloat16)
        low = (filtered - high.astype(jnp.float32)).astype(jnp.bfloat16)
        coefficient = jnp.dot(
            jnp.concatenate([high, low], axis=1), fwd_ref[dict_index], preferred_element_type=jnp.float32
        )
        for b in range(2):
            part = coefficient[:, b * columns : (b + 1) * columns].reshape(group, capacity, columns)
            combined = part + dual_ref[b, pick].astype(jnp.float32)
            u_ref[b, pick] = combined
            sq_ref[b] += jnp.sum(combined * combined, axis=0)
        return carry

    lax.fori_loop(0, channels // group, analyse, 0)

    keep = lax.broadcasted_iota(jnp.int32, (capacity, columns), 0) < length
    for b in range(2):
        radius = thr_ref[step * 2 + b]
        scale = radius / jnp.maximum(jnp.sqrt(sq_ref[b]), radius)
        sq_ref[b] = jnp.where(keep, scale, 0.0)

    def synthesise(i, carry):
        pick = pl.ds(i * group, group)
        parts = []
        for b in range(2):
            scaled = u_ref[b, pick] * sq_ref[b][None]
            next_ref[b, pick] = scaled.astype(jnp.bfloat16)
            parts.append(scaled.reshape(rows, columns).astype(jnp.bfloat16))
        z = jnp.dot(jnp.concatenate(parts, axis=1), adj_ref[dict_index], preferred_element_type=jnp.float32)
        z = z.reshape(group, capacity, columns)
        for h in range(2):
            z_ref[h, :, 8 : 8 + capacity, :] = z[:, :, h * LANES : (h + 1) * LANES]
        for h in range(2):
            total = taps[0] * z_ref[h, :, 8 : 8 + ext, :]
            for k in range(1, TAPS):
                total = total + taps[k] * z_ref[h, :, 8 - k : 8 - k + ext, :]
            merged_ref[pick, h * ext : (h + 1) * ext, :] += total

        return carry

    lax.fori_loop(0, channels // group, synthesise, 0)

    @pl.when(step == pl.num_programs(0) - 1)
    def _():
        spill_ref[...] = jnp.zeros_like(spill_ref)

        @pl.when(above == 1)
        def _():
            for h in range(2):
                spill_ref[:, ABOVE * h : ABOVE * (h + 1), :] = merged_ref[:, h * ext : h * ext + ABOVE, :]

        @pl.when(below == 1)
        def _():
            for h in range(2):
                spill_ref[:, ABOVE * h : ABOVE * h + 1, :] = merged_ref[:, pl.ds(h * ext + ABOVE + length, 1), :]


def border_kernel(ext, info_ref, merged_ref, spill_ref, out_ref, sem):
    length, below, above = info_ref[0], info_ref[1], info_ref[2]
    inside = info_ref[4].astype(jnp.float32)

    @pl.when(above == 1)
    def _():
        for h in range(2):
            merged_ref[:, h * ext : h * ext + ABOVE, :] = inside * spill_ref[:, ABOVE * h : ABOVE * (h + 1), :]

    @pl.when(below == 1)
    def _():
        for h in range(2):
            row = pl.ds(h * ext + ABOVE + length, 1)
            merged_ref[:, row, :] = inside * spill_ref[:, ABOVE * h : ABOVE * h + 1, :]

    copy = pltpu.make_async_copy(merged_ref, out_ref, sem)
    copy.start()
    copy.wait()


def on_device(image_cube, dual, lowpass, thresholds, facet_rows):
    band = lax.axis_index("grp")
    facet = lax.axis_index("fac")
    facets = lax.axis_size("fac")
    bands = lax.axis_size("grp")
    _, band_rows, columns = image_cube.shape
    subbands, channels, capacity, _ = dual.shape
    ext = capacity + TAPS
    per_step = 8
    strip_rows = MARGIN + band_rows + capacity
    lengths = lax.dynamic_index_in_dim(facet_rows, band, 0, keepdims=False)
    own_length = lax.dynamic_slice_in_dim(lengths, facet, 1)

    row_scratch = [
        pltpu.VMEM((2, strip_rows, LANES), jnp.float32),
        pltpu.SMEM((facets,), jnp.int32),
        pltpu.SemaphoreType.DMA((2,)),
    ]
    blocks = pl.BlockSpec((per_step, 2 * ext, LANES), lambda i, *_: (i, 0, 0))
    smem = pl.BlockSpec(memory_space=pltpu.SMEM)
    vmem = pl.BlockSpec(memory_space=pltpu.VMEM)
    hbm = pl.BlockSpec(memory_space=pltpu.HBM)
    packed = pl.pallas_call(
        functools.partial(pack_kernel, per_step, ext),
        out_shape=pltpu.HBM((facets, 2 * ext, LANES), jnp.float32),
        in_specs=[smem, hbm],
        out_specs=hbm,
        scratch_shapes=row_scratch[:2] + [
            pltpu.VMEM((facets, 2 * ext, LANES), jnp.float32),
            pltpu.SemaphoreType.DMA((2,)),
            pltpu.SemaphoreType.DMA((facets // per_step,)),
        ],
        compiler_params=pltpu.CompilerParams(vmem_limit_bytes=16 << 20),
        name="pack_facets",
    )(facet_rows, pltpu.with_memory_space_constraint(image_cube, pltpu.HBM))

    received = lax.all_to_all(packed, "fac", split_axis=0, concat_axis=0, tiled=True)

    taps = filter_taps(lowpass)
    matrices = column_matrices(taps, columns)
    forward = jnp.concatenate([matrices[:, 0], matrices[:, 1]], axis=2)
    forward = jnp.concatenate([forward, forward], axis=1)
    swapped = jnp.swapaxes(matrices, 2, 3)
    adjoint = jnp.concatenate([swapped[:, 0], swapped[:, 1]], axis=1)
    group = 16
    steps = subbands // 2
    pair = pl.BlockSpec((2, channels, capacity, columns), lambda i: (i, 0, 0, 0))
    below = facet == facets - 1
    above = facet == 0
    before = jnp.where(above, band > 0, band < bands - 1)
    after = jnp.where(above, band < bands - 1, band > 0)
    flags = [flag.astype(jnp.int32) for flag in (below, above, before, after)]
    info = jnp.stack([own_length[0]] + flags)
    edge_row = jnp.where(above, 0, own_length[0] + ABOVE)
    edges = [lax.dynamic_slice_in_dim(received, h * ext + edge_row, ABOVE, 1) for h in range(2)]
    edges = border_shift(jnp.concatenate(edges, axis=1), bands, facets, 1)
    dual_next, merged, spill = pl.pallas_call(
        functools.partial(facet_kernel, group, ext),
        grid=(steps,),
        out_shape=(
            jax.ShapeDtypeStruct(dual.shape, jnp.bfloat16),
            jax.ShapeDtypeStruct(received.shape, jnp.float32),
            jax.ShapeDtypeStruct(edges.shape, jnp.float32),
        ),
        in_specs=[
            smem, smem, smem, vmem, hbm, pair,
            pl.BlockSpec(forward.shape, lambda i: (0, 0, 0)),
            pl.BlockSpec(adjoint.shape, lambda i: (0, 0, 0)),
        ],
        out_specs=(pair, vmem, vmem),
        scratch_shapes=[
            pltpu.VMEM((channels, 2 * ext, LANES), jnp.float32),
            pltpu.VMEM((2, channels, capacity, columns), jnp.float32),
            pltpu.VMEM((2, capacity, columns), jnp.float32),
            pltpu.VMEM((2, group, capacity + 16, LANES), jnp.float32),
            pltpu.SemaphoreType.DMA((channels // group,)),
        ],
        compiler_params=pltpu.CompilerParams(vmem_limit_bytes=44 << 20),
        name="facet_update",
    )(taps.reshape(-1), thresholds, info, edges, received, dual, forward, adjoint)

    spill = border_shift(spill, bands, facets, -1)
    merged = pl.pallas_call(
        functools.partial(border_kernel, ext),
        out_shape=pltpu.HBM(received.shape, jnp.float32),
        in_specs=[smem, vmem, vmem],
        out_specs=hbm,
        scratch_shapes=[pltpu.SemaphoreType.DMA],
        compiler_params=pltpu.CompilerParams(vmem_limit_bytes=16 << 20),
        name="add_border_rows",
    )(info, merged, spill)
    returned = lax.all_to_all(merged, "fac", split_axis=0, concat_axis=0, tiled=True)

    prior_term = pl.pallas_call(
        functools.partial(unpack_kernel, per_step, ext),
        grid=(facets // per_step,),
        out_shape=jax.ShapeDtypeStruct(image_cube.shape, jnp.float32),
        in_specs=[smem, blocks],
        out_specs=hbm,
        scratch_shapes=row_scratch,
        compiler_params=pltpu.CompilerParams(vmem_limit_bytes=16 << 20),
        name="unpack_facets",
    )(facet_rows, returned)
    return dual_next, prior_term


def solution(mesh):
    placed = (P("fac", "grp", None), P(None, None, ("grp", "fac"), None), P(), P(), P())
    return jax.shard_map(
        on_device,
        mesh=mesh,
        in_specs=placed,
        out_specs=(P(None, None, ("grp", "fac"), None), P("fac", "grp", None)),
        check_vma=False,
    )
```

```python
import functools

import jax
import jax.numpy as jnp
from jax import lax
from jax.experimental import pallas as pl
from jax.experimental.pallas import tpu as pltpu
from jax.sharding import PartitionSpec as P

TAPS = 4
ABOVE = 2
MARGIN = 8
LANES = 128


def border_shift(x, bands, facets, by):
    pairs = []
    for b in range(bands):
        for facet in range(facets):
            to = b + by if facet % 2 == 0 else b - by
            pairs.append((b * facets + facet, (to % bands) * facets + facet))
    return lax.ppermute(x, ("grp", "fac"), pairs)


def filter_taps(lowpass):
    low = lowpass.astype(jnp.float32)
    parity = jnp.where(jnp.arange(TAPS) % 2 == 0, 1.0, -1.0).astype(jnp.float32)
    return jnp.stack([low, parity * low[:, ::-1]], axis=1)


def column_matrices(taps, columns):
    row = jnp.arange(columns)[:, None]
    col = jnp.arange(columns)[None, :]
    offset = row - col + 2
    total = 0.0
    for k in range(TAPS):
        hit = (offset == k)[None, None]
        total = total + jnp.where(hit, taps[:, :, k, None, None], 0.0)
    return total.astype(jnp.bfloat16)


def facet_starts(rows_ref, starts_ref, facets):
    band = lax.axis_index("grp")

    def step(q, total):
        starts_ref[q] = total
        return total + rows_ref[band, q]

    lax.fori_loop(0, facets, step, jnp.int32(0))


def pack_kernel(per_copy, ext, rows_ref, image_ref, out_ref, strip, starts, blocks, in_sem, out_sem):
    band_rows = image_ref.shape[1]
    facets = rows_ref.shape[1]
    copies = [
        pltpu.make_async_copy(
            image_ref.at[0, :, pl.ds(h * LANES, LANES)], strip.at[h, pl.ds(MARGIN, band_rows)], in_sem.at[h]
        )
        for h in range(2)
    ]
    for copy in copies:
        copy.start()
    facet_starts(rows_ref, starts, facets)
    end = MARGIN + band_rows
    for h in range(2):
        strip[h, 0:MARGIN] = jnp.zeros((MARGIN, LANES), jnp.float32)
        strip[h, end:] = jnp.zeros((strip.shape[1] - end, LANES), jnp.float32)
    for copy in copies:
        copy.wait()
    for h in range(2):
        strip[h, MARGIN - ABOVE : MARGIN] = strip[h, end - ABOVE : end]
        strip[h, end : end + 1] = strip[h, MARGIN : MARGIN + 1]

    outs = []
    for g in range(facets // per_copy):
        for q in range(g * per_copy, (g + 1) * per_copy):
            begin = starts[q] + (MARGIN - ABOVE)
            for h in range(2):
                blocks[q, h * ext : (h + 1) * ext] = strip[h, pl.ds(begin, ext)]
        pick = pl.ds(g * per_copy, per_copy)
        outs.append(pltpu.make_async_copy(blocks.at[pick], out_ref.at[pick], out_sem.at[g]))
        outs[-1].start()
    for copy in outs:
        copy.wait()


def unpack_kernel(per_step, ext, rows_ref, block_ref, out_ref, strip, starts, sem):
    step = pl.program_id(0)
    band_rows = out_ref.shape[1]
    facets = rows_ref.shape[1]

    @pl.when(step == 0)
    def _():
        facet_starts(rows_ref, starts, facets)
        for h in range(2):
            strip[h, 0 : 2 * MARGIN] = jnp.zeros((2 * MARGIN, LANES), jnp.float32)

    shared = lax.broadcasted_iota(jnp.int32, (8, LANES), 0) < 3
    for q in range(per_step):
        begin = starts[step * per_step + q] + (MARGIN - ABOVE)
        for h in range(2):
            before = strip[h, pl.ds(begin, 8)]
            strip[h, pl.ds(begin, 8)] = block_ref[q, h * ext : h * ext + 8] + jnp.where(shared, before, 0.0)
            strip[h, pl.ds(begin + 8, ext - 8)] = block_ref[q, h * ext + 8 : (h + 1) * ext]

    @pl.when(step == pl.num_programs(0) - 1)
    def _():
        copies = []
        end = MARGIN + band_rows
        for h in range(2):
            strip[h, end - ABOVE : end] += strip[h, MARGIN - ABOVE : MARGIN]
            strip[h, MARGIN : MARGIN + 1] += strip[h, end : end + 1]
            copies.append(
                pltpu.make_async_copy(
                    strip.at[h, pl.ds(MARGIN, band_rows)],
                    out_ref.at[0, :, pl.ds(h * LANES, LANES)],
                    sem.at[h],
                )
            )
        for copy in copies:
            copy.start()
        for copy in copies:
            copy.wait()


def facet_kernel(group, ext, taps_ref, thr_ref, info_ref, edge_ref, x_hbm, dual_ref, fwd_ref, adj_ref,
                 next_ref, merged_ref, spill_ref, x_ref, u_ref, sq_ref, z_ref, in_sem):
    step = pl.program_id(0)
    channels, capacity, columns = dual_ref.shape[1:]
    dict_index = step // 2
    taps = [taps_ref[step * TAPS + k] for k in range(TAPS)]
    rows = group * capacity
    length, below, above = info_ref[0], info_ref[1], info_ref[2]
    inside = info_ref[3].astype(jnp.float32)

    def incoming(i):
        pick = pl.ds(i * group, group)
        return pltpu.make_async_copy(x_hbm.at[pick], x_ref.at[pick], in_sem.at[i])

    @pl.when(step == 0)
    def _():
        for i in range(channels // group):
            incoming(i).start()
        merged_ref[...] = jnp.zeros_like(merged_ref)
        z_ref[...] = jnp.zeros_like(z_ref)

    sq_ref[...] = jnp.zeros_like(sq_ref)

    def analyse(i, carry):
        pick = pl.ds(i * group, group)

        @pl.when(step == 0)
        def _():
            incoming(i).wait()

            @pl.when(above == 1)
            def _():
                for h in range(2):
                    x_ref[pick, h * ext : h * ext + ABOVE, :] = inside * edge_ref[pick, ABOVE * h : ABOVE * (h + 1), :]

            @pl.when(below == 1)
            def _():
                for h in range(2):
                    row = pl.ds(h * ext + ABOVE + length, 1)
                    x_ref[pick, row, :] = inside * edge_ref[pick, ABOVE * h : ABOVE * h + 1, :]

        halves = []
        for h in range(2):
            total = taps[0] * x_ref[pick, h * ext : h * ext + capacity, :]
            for k in range(1, TAPS):
                total = total + taps[k] * x_ref[pick, h * ext + k : h * ext + k + capacity, :]
            halves.append(total.reshape(rows, LANES))
        filtered = jnp.concatenate(halves, axis=1)
        high = filtered.astype(jnp.bfloat16)
        low = (filtered - high.astype(jnp.float32)).astype(jnp.bfloat16)
        coefficient = jnp.dot(
            jnp.concatenate([high, low], axis=1), fwd_ref[dict_index], preferred_element_type=jnp.float32
        )
        for b in range(2):
            part = coefficient[:, b * columns : (b + 1) * columns].reshape(group, capacity, columns)
            combined = part + dual_ref[b, pick].astype(jnp.float32)
            u_ref[b, pick] = combined
            sq_ref[b] += jnp.sum(combined * combined, axis=0)
        return carry

    lax.fori_loop(0, channels // group, analyse, 0)

    keep = lax.broadcasted_iota(jnp.int32, (capacity, columns), 0) < length
    for b in range(2):
        radius = thr_ref[step * 2 + b]
        scale = radius / jnp.maximum(jnp.sqrt(sq_ref[b]), radius)
        sq_ref[b] = jnp.where(keep, scale, 0.0)

    def synthesise(i, carry):
        pick = pl.ds(i * group, group)
        parts = []
        for b in range(2):
            scaled = u_ref[b, pick] * sq_ref[b][None]
            next_ref[b, pick] = scaled.astype(jnp.bfloat16)
            parts.append(scaled.reshape(rows, columns).astype(jnp.bfloat16))
        z = jnp.dot(jnp.concatenate(parts, axis=1), adj_ref[dict_index], preferred_element_type=jnp.float32)
        z = z.reshape(group, capacity, columns)
        for h in range(2):
            z_ref[h, :, 8 : 8 + capacity, :] = z[:, :, h * LANES : (h + 1) * LANES]
        for h in range(2):
            total = taps[0] * z_ref[h, :, 8 : 8 + ext, :]
            for k in range(1, TAPS):
                total = total + taps[k] * z_ref[h, :, 8 - k : 8 - k + ext, :]
            merged_ref[pick, h * ext : (h + 1) * ext, :] += total

        return carry

    lax.fori_loop(0, channels // group, synthesise, 0)

    @pl.when(step == pl.num_programs(0) - 1)
    def _():
        spill_ref[...] = jnp.zeros_like(spill_ref)

        @pl.when(above == 1)
        def _():
            for h in range(2):
                spill_ref[:, ABOVE * h : ABOVE * (h + 1), :] = merged_ref[:, h * ext : h * ext + ABOVE, :]

        @pl.when(below == 1)
        def _():
            for h in range(2):
                spill_ref[:, ABOVE * h : ABOVE * h + 1, :] = merged_ref[:, pl.ds(h * ext + ABOVE + length, 1), :]


def border_kernel(ext, info_ref, sent_ref, spill_ref, merged_ref):
    length, below, above = info_ref[0], info_ref[1], info_ref[2]
    inside = info_ref[4].astype(jnp.float32)

    @pl.when(above == 1)
    def _():
        for h in range(2):
            merged_ref[:, h * ext : h * ext + ABOVE, :] = inside * spill_ref[:, ABOVE * h : ABOVE * (h + 1), :]

    @pl.when(below == 1)
    def _():
        for h in range(2):
            row = pl.ds(h * ext + ABOVE + length, 1)
            merged_ref[:, row, :] = inside * spill_ref[:, ABOVE * h : ABOVE * h + 1, :]


def on_device(image_cube, dual, lowpass, thresholds, facet_rows):
    band = lax.axis_index("grp")
    facet = lax.axis_index("fac")
    facets = lax.axis_size("fac")
    bands = lax.axis_size("grp")
    _, band_rows, columns = image_cube.shape
    subbands, channels, capacity, _ = dual.shape
    ext = capacity + TAPS
    per_step = 8
    strip_rows = MARGIN + band_rows + capacity
    lengths = lax.dynamic_index_in_dim(facet_rows, band, 0, keepdims=False)
    own_length = lax.dynamic_slice_in_dim(lengths, facet, 1)

    row_scratch = [
        pltpu.VMEM((2, strip_rows, LANES), jnp.float32),
        pltpu.SMEM((facets,), jnp.int32),
        pltpu.SemaphoreType.DMA((2,)),
    ]
    blocks = pl.BlockSpec((per_step, 2 * ext, LANES), lambda i, *_: (i, 0, 0))
    smem = pl.BlockSpec(memory_space=pltpu.SMEM)
    vmem = pl.BlockSpec(memory_space=pltpu.VMEM)
    hbm = pl.BlockSpec(memory_space=pltpu.HBM)
    packed = pl.pallas_call(
        functools.partial(pack_kernel, per_step, ext),
        out_shape=pltpu.HBM((facets, 2 * ext, LANES), jnp.float32),
        in_specs=[smem, hbm],
        out_specs=hbm,
        scratch_shapes=row_scratch[:2] + [
            pltpu.VMEM((facets, 2 * ext, LANES), jnp.float32),
            pltpu.SemaphoreType.DMA((2,)),
            pltpu.SemaphoreType.DMA((facets // per_step,)),
        ],
        compiler_params=pltpu.CompilerParams(vmem_limit_bytes=16 << 20),
        name="pack_facets",
    )(facet_rows, pltpu.with_memory_space_constraint(image_cube, pltpu.HBM))

    received = lax.all_to_all(packed, "fac", split_axis=0, concat_axis=0, tiled=True)

    taps = filter_taps(lowpass)
    matrices = column_matrices(taps, columns)
    forward = jnp.concatenate([matrices[:, 0], matrices[:, 1]], axis=2)
    forward = jnp.concatenate([forward, forward], axis=1)
    swapped = jnp.swapaxes(matrices, 2, 3)
    adjoint = jnp.concatenate([swapped[:, 0], swapped[:, 1]], axis=1)
    group = 16
    steps = subbands // 2
    pair = pl.BlockSpec((2, channels, capacity, columns), lambda i: (i, 0, 0, 0))
    below = facet == facets - 1
    above = facet == 0
    before = jnp.where(above, band > 0, band < bands - 1)
    after = jnp.where(above, band < bands - 1, band > 0)
    flags = [flag.astype(jnp.int32) for flag in (below, above, before, after)]
    info = jnp.stack([own_length[0]] + flags)
    edge_row = jnp.where(above, 0, own_length[0] + ABOVE)
    edges = [lax.dynamic_slice_in_dim(received, h * ext + edge_row, ABOVE, 1) for h in range(2)]
    edges = border_shift(jnp.concatenate(edges, axis=1), bands, facets, 1)
    dual_next, merged, spill = pl.pallas_call(
        functools.partial(facet_kernel, group, ext),
        grid=(steps,),
        out_shape=(
            jax.ShapeDtypeStruct(dual.shape, jnp.bfloat16),
            jax.ShapeDtypeStruct(received.shape, jnp.float32),
            jax.ShapeDtypeStruct(edges.shape, jnp.float32),
        ),
        in_specs=[
            smem, smem, smem, vmem, hbm, pair,
            pl.BlockSpec(forward.shape, lambda i: (0, 0, 0)),
            pl.BlockSpec(adjoint.shape, lambda i: (0, 0, 0)),
        ],
        out_specs=(pair, vmem, vmem),
        scratch_shapes=[
            pltpu.VMEM((channels, 2 * ext, LANES), jnp.float32),
            pltpu.VMEM((2, channels, capacity, columns), jnp.float32),
            pltpu.VMEM((2, capacity, columns), jnp.float32),
            pltpu.VMEM((2, group, capacity + 16, LANES), jnp.float32),
            pltpu.SemaphoreType.DMA((channels // group,)),
        ],
        compiler_params=pltpu.CompilerParams(vmem_limit_bytes=44 << 20),
        name="facet_update",
    )(taps.reshape(-1), thresholds, info, edges, received, dual, forward, adjoint)

    spill = border_shift(spill, bands, facets, -1)
    merged = pl.pallas_call(
        functools.partial(border_kernel, ext),
        out_shape=jax.ShapeDtypeStruct(received.shape, jnp.float32),
        in_specs=[smem, vmem, vmem],
        out_specs=vmem,
        input_output_aliases={1: 0},
        compiler_params=pltpu.CompilerParams(vmem_limit_bytes=16 << 20),
        name="add_border_rows",
    )(info, merged, spill)
    returned = lax.all_to_all(merged, "fac", split_axis=0, concat_axis=0, tiled=True)

    prior_term = pl.pallas_call(
        functools.partial(unpack_kernel, per_step, ext),
        grid=(facets // per_step,),
        out_shape=jax.ShapeDtypeStruct(image_cube.shape, jnp.float32),
        in_specs=[smem, blocks],
        out_specs=hbm,
        scratch_shapes=row_scratch,
        compiler_params=pltpu.CompilerParams(vmem_limit_bytes=16 << 20),
        name="unpack_facets",
    )(facet_rows, returned)
    return dual_next, prior_term


def solution(mesh):
    placed = (P("fac", "grp", None), P(None, None, ("grp", "fac"), None), P(), P(), P())
    return jax.shard_map(
        on_device,
        mesh=mesh,
        in_specs=placed,
        out_specs=(P(None, None, ("grp", "fac"), None), P("fac", "grp", None)),
        check_vma=False,
    )
```

```python
import functools

import jax
import jax.numpy as jnp
from jax import lax
from jax.experimental import pallas as pl
from jax.experimental.pallas import tpu as pltpu
from jax.sharding import PartitionSpec as P

TAPS = 4
ABOVE = 2
MARGIN = 8
LANES = 128


def border_shift(x, bands, facets, by):
    pairs = []
    for b in range(bands):
        for facet in range(facets):
            to = b + by if facet % 2 == 0 else b - by
            pairs.append((b * facets + facet, (to % bands) * facets + facet))
    return lax.ppermute(x, ("grp", "fac"), pairs)


def filter_taps(lowpass):
    low = lowpass.astype(jnp.float32)
    parity = jnp.where(jnp.arange(TAPS) % 2 == 0, 1.0, -1.0).astype(jnp.float32)
    return jnp.stack([low, parity * low[:, ::-1]], axis=1)


def column_matrices(taps, columns):
    row = jnp.arange(columns)[:, None]
    col = jnp.arange(columns)[None, :]
    offset = row - col + 2
    total = 0.0
    for k in range(TAPS):
        hit = (offset == k)[None, None]
        total = total + jnp.where(hit, taps[:, :, k, None, None], 0.0)
    return total.astype(jnp.bfloat16)


def facet_starts(rows_ref, starts_ref, facets):
    band = lax.axis_index("grp")

    def step(q, total):
        starts_ref[q] = total
        return total + rows_ref[band, q]

    lax.fori_loop(0, facets, step, jnp.int32(0))


def pack_kernel(per_copy, ext, rows_hbm, image_ref, out_ref, strip, starts, rows_ref, blocks, in_sem, out_sem):
    band_rows = image_ref.shape[1]
    facets = rows_hbm.shape[1]
    steps = facets // per_copy
    fetch_rows = pltpu.make_async_copy(rows_hbm, rows_ref, in_sem.at[2 * steps])
    fetch_rows.start()
    part = band_rows // steps
    copies = [
        [
            pltpu.make_async_copy(
                image_ref.at[0, pl.ds(g * part, part), pl.ds(h * LANES, LANES)],
                strip.at[h, pl.ds(MARGIN + g * part, part)],
                in_sem.at[2 * g + h],
            )
            for h in range(2)
        ]
        for g in range(steps)
    ]
    for pair in copies[-1:] + copies[:-1]:
        for copy in pair:
            copy.start()
    end = MARGIN + band_rows
    for h in range(2):
        strip[h, 0:MARGIN] = jnp.zeros((MARGIN, LANES), jnp.float32)
        strip[h, end:] = jnp.zeros((strip.shape[1] - end, LANES), jnp.float32)
    fetch_rows.wait()
    facet_starts(rows_ref, starts, facets)

    def wait_for(g):
        for copy in copies[g]:
            copy.wait()

    wait_for(steps - 1)
    wait_for(0)
    for h in range(2):
        strip[h, MARGIN - ABOVE : MARGIN] = strip[h, end - ABOVE : end]
        strip[h, end : end + 1] = strip[h, MARGIN : MARGIN + 1]

    arrived = 1
    outs = []
    for g in range(steps):
        while arrived < steps - 1 and arrived * part < (g + 1) * per_copy * (ext - TAPS) + TAPS:
            wait_for(arrived)
            arrived += 1
        for q in range(g * per_copy, (g + 1) * per_copy):
            begin = starts[q] + (MARGIN - ABOVE)
            for h in range(2):
                blocks[q, h * ext : (h + 1) * ext] = strip[h, pl.ds(begin, ext)]
        pick = pl.ds(g * per_copy, per_copy)
        outs.append(pltpu.make_async_copy(blocks.at[pick], out_ref.at[pick], out_sem.at[g]))
        outs[-1].start()
    for copy in outs:
        copy.wait()


def unpack_kernel(per_step, ext, rows_ref, block_ref, out_ref, strip, starts, sem):
    step = pl.program_id(0)
    band_rows = out_ref.shape[1]
    facets = rows_ref.shape[1]

    @pl.when(step == 0)
    def _():
        facet_starts(rows_ref, starts, facets)
        for h in range(2):
            strip[h, 0 : 2 * MARGIN] = jnp.zeros((2 * MARGIN, LANES), jnp.float32)

    shared = lax.broadcasted_iota(jnp.int32, (8, LANES), 0) < 3
    for q in range(per_step):
        begin = starts[step * per_step + q] + (MARGIN - ABOVE)
        for h in range(2):
            before = strip[h, pl.ds(begin, 8)]
            strip[h, pl.ds(begin, 8)] = block_ref[q, h * ext : h * ext + 8] + jnp.where(shared, before, 0.0)
            strip[h, pl.ds(begin + 8, ext - 8)] = block_ref[q, h * ext + 8 : (h + 1) * ext]

    @pl.when(step == pl.num_programs(0) - 1)
    def _():
        copies = []
        end = MARGIN + band_rows
        for h in range(2):
            strip[h, end - ABOVE : end] += strip[h, MARGIN - ABOVE : MARGIN]
            strip[h, MARGIN : MARGIN + 1] += strip[h, end : end + 1]
            copies.append(
                pltpu.make_async_copy(
                    strip.at[h, pl.ds(MARGIN, band_rows)],
                    out_ref.at[0, :, pl.ds(h * LANES, LANES)],
                    sem.at[h],
                )
            )
        for copy in copies:
            copy.start()
        for copy in copies:
            copy.wait()


def facet_kernel(group, ext, taps_ref, thr_ref, info_ref, edge_ref, received_ref, dual_ref, fwd_ref, adj_ref,
                 next_ref, merged_ref, spill_ref, x_ref, u_ref, sq_ref, z_ref):
    step = pl.program_id(0)
    channels, capacity, columns = dual_ref.shape[1:]
    dict_index = step // 2
    taps = [taps_ref[step * TAPS + k] for k in range(TAPS)]
    rows = group * capacity
    length, below, above = info_ref[0], info_ref[1], info_ref[2]
    inside = info_ref[3].astype(jnp.float32)

    @pl.when(step == 0)
    def _():
        merged_ref[...] = jnp.zeros_like(merged_ref)
        z_ref[...] = jnp.zeros_like(z_ref)

        @pl.when(above == 1)
        def _():
            for h in range(2):
                x_ref[:, h * ext : h * ext + ABOVE, :] = inside * edge_ref[:, ABOVE * h : ABOVE * (h + 1), :]

        @pl.when(below == 1)
        def _():
            for h in range(2):
                row = pl.ds(h * ext + ABOVE + length, 1)
                x_ref[:, row, :] = inside * edge_ref[:, ABOVE * h : ABOVE * h + 1, :]

    sq_ref[...] = jnp.zeros_like(sq_ref)

    def analyse(i, begin, stop):
        pick = pl.ds(i * group, group)

        halves = []
        for h in range(2):
            total = taps[begin] * x_ref[pick, h * ext + begin : h * ext + begin + capacity, :]
            for k in range(begin + 1, stop):
                total = total + taps[k] * x_ref[pick, h * ext + k : h * ext + k + capacity, :]
            halves.append(total.reshape(rows, LANES))
        filtered = jnp.concatenate(halves, axis=1)
        high = filtered.astype(jnp.bfloat16)
        low = (filtered - high.astype(jnp.float32)).astype(jnp.bfloat16)
        coefficient = jnp.dot(
            jnp.concatenate([high, low], axis=1), fwd_ref[0], preferred_element_type=jnp.float32
        )
        for b in range(2):
            part = coefficient[:, b * columns : (b + 1) * columns].reshape(group, capacity, columns)
            combined = part + dual_ref[b, pick].astype(jnp.float32)
            u_ref[b, pick] = combined
            sq_ref[b] += jnp.sum(combined * combined, axis=0)

    def over_groups(work):
        @pl.when(dict_index == 0)
        def _():
            pl.loop(0, channels // group)(lambda i: work(i, 1, 3))

        @pl.when(dict_index > 0)
        def _():
            pl.loop(0, channels // group)(lambda i: work(i, 0, TAPS))

    over_groups(analyse)

    keep = lax.broadcasted_iota(jnp.int32, (capacity, columns), 0) < length
    for b in range(2):
        radius = thr_ref[step * 2 + b]
        scale = radius / jnp.maximum(jnp.sqrt(sq_ref[b]), radius)
        sq_ref[b] = jnp.where(keep, scale, 0.0)

    def synthesise(i, begin, stop):
        pick = pl.ds(i * group, group)
        parts = []
        for b in range(2):
            scaled = u_ref[b, pick] * sq_ref[b][None]
            next_ref[b, pick] = scaled.astype(jnp.bfloat16)
            parts.append(scaled.reshape(rows, columns).astype(jnp.bfloat16))
        z = jnp.dot(jnp.concatenate(parts, axis=1), adj_ref[0], preferred_element_type=jnp.float32)
        z = z.reshape(group, capacity, columns)
        for h in range(2):
            z_ref[h, :, 8 : 8 + capacity, :] = z[:, :, h * LANES : (h + 1) * LANES]
        for h in range(2):
            total = taps[begin] * z_ref[h, :, 8 - begin : 8 - begin + ext, :]
            for k in range(begin + 1, stop):
                total = total + taps[k] * z_ref[h, :, 8 - k : 8 - k + ext, :]
            merged_ref[pick, h * ext : (h + 1) * ext, :] += total

    over_groups(synthesise)

    @pl.when(step == pl.num_programs(0) - 1)
    def _():
        spill_ref[...] = jnp.zeros_like(spill_ref)

        @pl.when(above == 1)
        def _():
            for h in range(2):
                spill_ref[:, ABOVE * h : ABOVE * (h + 1), :] = merged_ref[:, h * ext : h * ext + ABOVE, :]

        @pl.when(below == 1)
        def _():
            for h in range(2):
                spill_ref[:, ABOVE * h : ABOVE * h + 1, :] = merged_ref[:, pl.ds(h * ext + ABOVE + length, 1), :]


def border_kernel(ext, info_ref, sent_ref, spill_ref, merged_ref):
    length, below, above = info_ref[0], info_ref[1], info_ref[2]
    inside = info_ref[4].astype(jnp.float32)

    @pl.when(above == 1)
    def _():
        for h in range(2):
            merged_ref[:, h * ext : h * ext + ABOVE, :] = inside * spill_ref[:, ABOVE * h : ABOVE * (h + 1), :]

    @pl.when(below == 1)
    def _():
        for h in range(2):
            row = pl.ds(h * ext + ABOVE + length, 1)
            merged_ref[:, row, :] = inside * spill_ref[:, ABOVE * h : ABOVE * h + 1, :]


def on_device(image_cube, dual, lowpass, thresholds, facet_rows):
    band = lax.axis_index("grp")
    facet = lax.axis_index("fac")
    facets = lax.axis_size("fac")
    bands = lax.axis_size("grp")
    _, band_rows, columns = image_cube.shape
    subbands, channels, capacity, _ = dual.shape
    ext = capacity + TAPS
    per_step = 8
    strip_rows = MARGIN + band_rows + capacity
    lengths = lax.dynamic_index_in_dim(facet_rows, band, 0, keepdims=False)
    own_length = lax.dynamic_slice_in_dim(lengths, facet, 1)

    row_scratch = [
        pltpu.VMEM((2, strip_rows, LANES), jnp.float32),
        pltpu.SMEM((facets,), jnp.int32),
        pltpu.SemaphoreType.DMA((2,)),
    ]
    blocks = pl.BlockSpec((per_step, 2 * ext, LANES), lambda i, *_: (i, 0, 0))
    smem = pl.BlockSpec(memory_space=pltpu.SMEM)
    vmem = pl.BlockSpec(memory_space=pltpu.VMEM)
    hbm = pl.BlockSpec(memory_space=pltpu.HBM)
    packed = pl.pallas_call(
        functools.partial(pack_kernel, per_step, ext),
        out_shape=pltpu.HBM((facets, 2 * ext, LANES), jnp.float32),
        in_specs=[hbm, hbm],
        out_specs=hbm,
        scratch_shapes=row_scratch[:2] + [
            pltpu.SMEM(facet_rows.shape, jnp.int32),
            pltpu.VMEM((facets, 2 * ext, LANES), jnp.float32),
            pltpu.SemaphoreType.DMA((2 * (facets // per_step) + 1,)),
            pltpu.SemaphoreType.DMA((facets // per_step,)),
        ],
        compiler_params=pltpu.CompilerParams(vmem_limit_bytes=16 << 20),
        name="pack_facets",
    )(*(pltpu.with_memory_space_constraint(a, pltpu.HBM) for a in (facet_rows, image_cube)))

    received = lax.all_to_all(packed, "fac", split_axis=0, concat_axis=0, tiled=True)

    taps = filter_taps(lowpass)
    matrices = column_matrices(taps, columns)
    forward = jnp.concatenate([matrices[:, 0], matrices[:, 1]], axis=2)
    forward = jnp.concatenate([forward, forward], axis=1)
    swapped = jnp.swapaxes(matrices, 2, 3)
    adjoint = jnp.concatenate([swapped[:, 0], swapped[:, 1]], axis=1)
    group = 16
    steps = subbands // 2
    pair = pl.BlockSpec((2, channels, capacity, columns), lambda i: (i, 0, 0, 0))
    below = facet == facets - 1
    above = facet == 0
    before = jnp.where(above, band > 0, band < bands - 1)
    after = jnp.where(above, band < bands - 1, band > 0)
    flags = [flag.astype(jnp.int32) for flag in (below, above, before, after)]
    info = jnp.stack([own_length[0]] + flags)
    edge_row = jnp.where(above, 0, own_length[0] + ABOVE)
    edges = [lax.dynamic_slice_in_dim(received, h * ext + edge_row, ABOVE, 1) for h in range(2)]
    edges = border_shift(jnp.concatenate(edges, axis=1), bands, facets, 1)
    dual_next, merged, spill, _ = pl.pallas_call(
        functools.partial(facet_kernel, group, ext),
        grid=(steps,),
        out_shape=(
            jax.ShapeDtypeStruct(dual.shape, jnp.bfloat16),
            jax.ShapeDtypeStruct(received.shape, jnp.float32),
            jax.ShapeDtypeStruct(edges.shape, jnp.float32),
            jax.ShapeDtypeStruct(received.shape, jnp.float32),
        ),
        in_specs=[
            smem, smem, smem, vmem, vmem, pair,
            pl.BlockSpec((1,) + forward.shape[1:], lambda i: (i // 2, 0, 0)),
            pl.BlockSpec((1,) + adjoint.shape[1:], lambda i: (i // 2, 0, 0)),
        ],
        out_specs=(pair, vmem, vmem, vmem),
        input_output_aliases={4: 3},
        scratch_shapes=[
            pltpu.VMEM((2, channels, capacity, columns), jnp.float32),
            pltpu.VMEM((2, capacity, columns), jnp.float32),
            pltpu.VMEM((2, group, capacity + 16, LANES), jnp.float32),
        ],
        compiler_params=pltpu.CompilerParams(vmem_limit_bytes=44 << 20),
        name="facet_update",
    )(taps.reshape(-1), thresholds, info, edges, received, dual, forward, adjoint)

    spill = border_shift(spill, bands, facets, -1)
    merged = pl.pallas_call(
        functools.partial(border_kernel, ext),
        out_shape=jax.ShapeDtypeStruct(received.shape, jnp.float32),
        in_specs=[smem, vmem, vmem],
        out_specs=vmem,
        input_output_aliases={1: 0},
        compiler_params=pltpu.CompilerParams(vmem_limit_bytes=16 << 20),
        name="add_border_rows",
    )(info, merged, spill)
    returned = lax.all_to_all(merged, "fac", split_axis=0, concat_axis=0, tiled=True)

    prior_term = pl.pallas_call(
        functools.partial(unpack_kernel, per_step, ext),
        grid=(facets // per_step,),
        out_shape=jax.ShapeDtypeStruct(image_cube.shape, jnp.float32),
        in_specs=[smem, blocks],
        out_specs=hbm,
        scratch_shapes=row_scratch,
        compiler_params=pltpu.CompilerParams(vmem_limit_bytes=16 << 20),
        name="unpack_facets",
    )(facet_rows, returned)
    return dual_next, prior_term


def solution(mesh):
    placed = (P("fac", "grp", None), P(None, None, ("grp", "fac"), None), P(), P(), P())
    return jax.shard_map(
        on_device,
        mesh=mesh,
        in_specs=placed,
        out_specs=(P(None, None, ("grp", "fac"), None), P("fac", "grp", None)),
        check_vma=False,
    )
```

```python
import functools

import jax
import jax.numpy as jnp
from jax import lax
from jax.experimental import pallas as pl
from jax.experimental.pallas import tpu as pltpu
from jax.sharding import PartitionSpec as P

TAPS = 4
ABOVE = 2
MARGIN = 8
LANES = 128


def border_shift(x, bands, facets, by):
    pairs = []
    for b in range(bands):
        for facet in range(facets):
            to = b + by if facet % 2 == 0 else b - by
            pairs.append((b * facets + facet, (to % bands) * facets + facet))
    return lax.ppermute(x, ("grp", "fac"), pairs)


def filter_taps(lowpass):
    low = lowpass.astype(jnp.float32)
    parity = jnp.where(jnp.arange(TAPS) % 2 == 0, 1.0, -1.0).astype(jnp.float32)
    return jnp.stack([low, parity * low[:, ::-1]], axis=1)


def column_matrices(taps, columns):
    row = jnp.arange(columns)[:, None]
    col = jnp.arange(columns)[None, :]
    offset = row - col + 2
    total = 0.0
    for k in range(TAPS):
        hit = (offset == k)[None, None]
        total = total + jnp.where(hit, taps[:, :, k, None, None], 0.0)
    return total.astype(jnp.bfloat16)


def facet_starts(rows_ref, starts_ref, facets):
    band = lax.axis_index("grp")

    def step(q, total):
        starts_ref[q] = total
        return total + rows_ref[band, q]

    lax.fori_loop(0, facets, step, jnp.int32(0))


def pack_kernel(per_copy, ext, rows_hbm, image_ref, out_ref, strip, starts, rows_ref, blocks, in_sem, out_sem):
    band_rows = image_ref.shape[1]
    facets = rows_hbm.shape[1]
    steps = facets // per_copy
    fetch_rows = pltpu.make_async_copy(rows_hbm, rows_ref, in_sem.at[2 * steps])
    fetch_rows.start()
    part = band_rows // steps
    copies = [
        [
            pltpu.make_async_copy(
                image_ref.at[0, pl.ds(g * part, part), pl.ds(h * LANES, LANES)],
                strip.at[h, pl.ds(MARGIN + g * part, part)],
                in_sem.at[2 * g + h],
            )
            for h in range(2)
        ]
        for g in range(steps)
    ]
    for pair in copies[-1:] + copies[:-1]:
        for copy in pair:
            copy.start()
    end = MARGIN + band_rows
    for h in range(2):
        strip[h, 0:MARGIN] = jnp.zeros((MARGIN, LANES), jnp.float32)
        strip[h, end:] = jnp.zeros((strip.shape[1] - end, LANES), jnp.float32)
    fetch_rows.wait()
    facet_starts(rows_ref, starts, facets)

    def wait_for(g):
        for copy in copies[g]:
            copy.wait()

    wait_for(steps - 1)
    wait_for(0)
    for h in range(2):
        strip[h, MARGIN - ABOVE : MARGIN] = strip[h, end - ABOVE : end]
        strip[h, end : end + 1] = strip[h, MARGIN : MARGIN + 1]

    arrived = 1
    outs = []
    for g in range(steps):
        while arrived < steps - 1 and arrived * part < (g + 1) * per_copy * (ext - TAPS) + TAPS:
            wait_for(arrived)
            arrived += 1
        for q in range(g * per_copy, (g + 1) * per_copy):
            begin = starts[q] + (MARGIN - ABOVE)
            for h in range(2):
                blocks[q, h * ext : (h + 1) * ext] = strip[h, pl.ds(begin, ext)]
        pick = pl.ds(g * per_copy, per_copy)
        outs.append(pltpu.make_async_copy(blocks.at[pick], out_ref.at[pick], out_sem.at[g]))
        outs[-1].start()
    for copy in outs:
        copy.wait()


def unpack_kernel(capacity, ext, rows_ref, block_ref, out_ref, strip, starts, sem):
    band_rows = out_ref.shape[1]
    facets = block_ref.shape[0]
    end = MARGIN + band_rows
    facet_starts(rows_ref, starts, facets)
    for h in range(2):
        strip[h, 0 : 2 * MARGIN] = jnp.zeros((2 * MARGIN, LANES), jnp.float32)

    copies = []

    def send(begin, stop):
        for h in range(2):
            copies.append(
                pltpu.make_async_copy(
                    strip.at[h, pl.ds(MARGIN + begin, stop - begin)],
                    out_ref.at[0, pl.ds(begin, stop - begin), pl.ds(h * LANES, LANES)],
                    sem.at[len(copies)],
                )
            )
            copies[-1].start()

    shared = lax.broadcasted_iota(jnp.int32, (8, LANES), 0) < 3
    early = 3 * facets // 4
    ready = (band_rows - (facets - early) * capacity) // 8 * 8 - 8
    for q in range(facets):
        if q == early:
            send(8, ready)
        begin = starts[q] + (MARGIN - ABOVE)
        for h in range(2):
            before = strip[h, pl.ds(begin, 8)]
            strip[h, pl.ds(begin, 8)] = block_ref[q, h * ext : h * ext + 8] + jnp.where(shared, before, 0.0)
            strip[h, pl.ds(begin + 8, ext - 8)] = block_ref[q, h * ext + 8 : (h + 1) * ext]
    for h in range(2):
        strip[h, end - ABOVE : end] += strip[h, MARGIN - ABOVE : MARGIN]
        strip[h, MARGIN : MARGIN + 1] += strip[h, end : end + 1]
    send(0, 8)
    send(ready, band_rows)
    for copy in copies:
        copy.wait()


def stage_kernel(received_ref, dual_hbm, fwd_any, adj_any, first_ref, fwd_ref, adj_ref, sem):
    pairs = ((dual_hbm.at[pl.ds(0, 2)], first_ref), (fwd_any, fwd_ref), (adj_any, adj_ref))
    copies = [pltpu.make_async_copy(src, dst, sem.at[i]) for i, (src, dst) in enumerate(pairs)]
    for copy in copies:
        copy.start()
    for copy in copies:
        copy.wait()


def tail_kernel(tail_ref, begun_hbm, next_hbm, done_ref, sem):
    pair = tail_ref.shape[0]
    copy = pltpu.make_async_copy(tail_ref, next_hbm.at[pl.ds(next_hbm.shape[0] - pair, pair)], sem)
    copy.start()
    done_ref[...] = jnp.zeros_like(done_ref)
    copy.wait()


def facet_kernel(group, ext, taps_ref, thr_ref, info_ref, edge_ref, received_ref, first_ref, dual_hbm, fwd_ref, adj_ref,
                 next_hbm, tail_ref, merged_ref, spill_ref, x_ref,
                 in_slots, out_slots, u_ref, sq_ref, z_ref, in_sem, out_sem):
    step = pl.program_id(0)
    steps = dual_hbm.shape[0] // 2
    channels, capacity, columns = dual_hbm.shape[1:]
    slot = lax.rem(step, 2)

    def fetch(i, place):
        return pltpu.make_async_copy(dual_hbm.at[pl.ds(2 * i, 2)], in_slots.at[place], in_sem.at[place])

    def store(i, place):
        return pltpu.make_async_copy(out_slots.at[place], next_hbm.at[pl.ds(2 * i, 2)], out_sem.at[place])

    @pl.when(step > 0)
    def _():
        fetch(step, slot).wait()

    @pl.when(step < steps - 1)
    def _():
        fetch(step + 1, 1 - slot).start()

    dict_index = step // 2
    taps = [taps_ref[step * TAPS + k] for k in range(TAPS)]
    rows = group * capacity
    length, below, above = info_ref[0], info_ref[1], info_ref[2]
    inside = info_ref[3].astype(jnp.float32)

    @pl.when(step == 0)
    def _():
        merged_ref[...] = jnp.zeros_like(merged_ref)
        z_ref[...] = jnp.zeros_like(z_ref)

        @pl.when(above == 1)
        def _():
            for h in range(2):
                x_ref[:, h * ext : h * ext + ABOVE, :] = inside * edge_ref[:, ABOVE * h : ABOVE * (h + 1), :]

        @pl.when(below == 1)
        def _():
            for h in range(2):
                row = pl.ds(h * ext + ABOVE + length, 1)
                x_ref[:, row, :] = inside * edge_ref[:, ABOVE * h : ABOVE * h + 1, :]

    sq_ref[...] = jnp.zeros_like(sq_ref)

    def analyse(i, source, begin, stop):
        pick = pl.ds(i * group, group)

        halves = []
        for h in range(2):
            total = taps[begin] * x_ref[pick, h * ext + begin : h * ext + begin + capacity, :]
            for k in range(begin + 1, stop):
                total = total + taps[k] * x_ref[pick, h * ext + k : h * ext + k + capacity, :]
            halves.append(total.reshape(rows, LANES))
        filtered = jnp.concatenate(halves, axis=1)
        high = filtered.astype(jnp.bfloat16)
        low = (filtered - high.astype(jnp.float32)).astype(jnp.bfloat16)
        coefficient = jnp.dot(
            jnp.concatenate([high, low], axis=1), fwd_ref[dict_index], preferred_element_type=jnp.float32
        )
        for b in range(2):
            part = coefficient[:, b * columns : (b + 1) * columns].reshape(group, capacity, columns)
            combined = part + source[b, pick].astype(jnp.float32)
            u_ref[b, pick] = combined
            sq_ref[b] += jnp.sum(combined * combined, axis=0)

    def over_groups(when, work, place, begin, stop):
        @pl.when(when)
        def _():
            pl.loop(0, channels // group)(lambda i: work(i, place, begin, stop))

    over_groups(step == 0, analyse, first_ref, 1, 3)
    over_groups(step == 1, analyse, in_slots.at[1], 1, 3)
    over_groups(step >= 2, analyse, in_slots.at[slot], 0, TAPS)

    keep = lax.broadcasted_iota(jnp.int32, (capacity, columns), 0) < length
    for b in range(2):
        radius = thr_ref[step * 2 + b]
        scale = radius / jnp.maximum(jnp.sqrt(sq_ref[b]), radius)
        sq_ref[b] = jnp.where(keep, scale, 0.0)

    def synthesise(i, target, begin, stop):
        pick = pl.ds(i * group, group)
        parts = []
        for b in range(2):
            scaled = u_ref[b, pick] * sq_ref[b][None]
            target[b, pick] = scaled.astype(jnp.bfloat16)
            parts.append(scaled.reshape(rows, columns).astype(jnp.bfloat16))
        z = jnp.dot(jnp.concatenate(parts, axis=1), adj_ref[dict_index], preferred_element_type=jnp.float32)
        z = z.reshape(group, capacity, columns)
        for h in range(2):
            z_ref[h, :, 8 : 8 + capacity, :] = z[:, :, h * LANES : (h + 1) * LANES]
        for h in range(2):
            total = taps[begin] * z_ref[h, :, 8 - begin : 8 - begin + ext, :]
            for k in range(begin + 1, stop):
                total = total + taps[k] * z_ref[h, :, 8 - k : 8 - k + ext, :]
            merged_ref[pick, h * ext : (h + 1) * ext, :] += total

    @pl.when(step == 2)
    def _():
        store(0, 0).wait()

    over_groups(step < 2, synthesise, out_slots.at[slot], 1, 3)
    over_groups(jnp.logical_and(step >= 2, step < steps - 1), synthesise, out_slots.at[slot], 0, TAPS)
    over_groups(step == steps - 1, synthesise, tail_ref, 0, TAPS)

    @pl.when(step < steps - 1)
    def _():
        store(step, slot).start()

    @pl.when(step == pl.num_programs(0) - 1)
    def _():
        spill_ref[...] = jnp.zeros_like(spill_ref)

        @pl.when(above == 1)
        def _():
            for h in range(2):
                spill_ref[:, ABOVE * h : ABOVE * (h + 1), :] = merged_ref[:, h * ext : h * ext + ABOVE, :]

        @pl.when(below == 1)
        def _():
            for h in range(2):
                spill_ref[:, ABOVE * h : ABOVE * h + 1, :] = merged_ref[:, pl.ds(h * ext + ABOVE + length, 1), :]

        store(1, 1).wait()
        store(2, 0).wait()


def border_kernel(ext, info_ref, sent_ref, spill_ref, stored_ref, merged_ref):
    length, below, above = info_ref[0], info_ref[1], info_ref[2]
    inside = info_ref[4].astype(jnp.float32)

    @pl.when(above == 1)
    def _():
        for h in range(2):
            merged_ref[:, h * ext : h * ext + ABOVE, :] = inside * spill_ref[:, ABOVE * h : ABOVE * (h + 1), :]

    @pl.when(below == 1)
    def _():
        for h in range(2):
            row = pl.ds(h * ext + ABOVE + length, 1)
            merged_ref[:, row, :] = inside * spill_ref[:, ABOVE * h : ABOVE * h + 1, :]


def on_device(image_cube, dual, lowpass, thresholds, facet_rows):
    band = lax.axis_index("grp")
    facet = lax.axis_index("fac")
    facets = lax.axis_size("fac")
    bands = lax.axis_size("grp")
    _, band_rows, columns = image_cube.shape
    subbands, channels, capacity, _ = dual.shape
    ext = capacity + TAPS
    per_step = 8
    strip_rows = MARGIN + band_rows + capacity
    lengths = lax.dynamic_index_in_dim(facet_rows, band, 0, keepdims=False)
    own_length = lax.dynamic_slice_in_dim(lengths, facet, 1)

    row_scratch = [
        pltpu.VMEM((2, strip_rows, LANES), jnp.float32),
        pltpu.SMEM((facets,), jnp.int32),
    ]
    smem = pl.BlockSpec(memory_space=pltpu.SMEM)
    vmem = pl.BlockSpec(memory_space=pltpu.VMEM)
    hbm = pl.BlockSpec(memory_space=pltpu.HBM)
    packed = pl.pallas_call(
        functools.partial(pack_kernel, per_step, ext),
        out_shape=pltpu.HBM((facets, 2 * ext, LANES), jnp.float32),
        in_specs=[hbm, hbm],
        out_specs=hbm,
        scratch_shapes=row_scratch[:2] + [
            pltpu.SMEM(facet_rows.shape, jnp.int32),
            pltpu.VMEM((facets, 2 * ext, LANES), jnp.float32),
            pltpu.SemaphoreType.DMA((2 * (facets // per_step) + 1,)),
            pltpu.SemaphoreType.DMA((facets // per_step,)),
        ],
        compiler_params=pltpu.CompilerParams(vmem_limit_bytes=16 << 20),
        name="pack_facets",
    )(*(pltpu.with_memory_space_constraint(a, pltpu.HBM) for a in (facet_rows, image_cube)))

    received = lax.all_to_all(packed, "fac", split_axis=0, concat_axis=0, tiled=True)

    taps = filter_taps(lowpass)
    matrices = column_matrices(taps, columns)
    forward = jnp.concatenate([matrices[:, 0], matrices[:, 1]], axis=2)
    forward = jnp.concatenate([forward, forward], axis=1)
    swapped = jnp.swapaxes(matrices, 2, 3)
    adjoint = jnp.concatenate([swapped[:, 0], swapped[:, 1]], axis=1)
    group = 16
    dual = pltpu.with_memory_space_constraint(dual, pltpu.HBM)
    pair = (2,) + dual.shape[1:]
    any_space = pl.BlockSpec(memory_space=pl.ANY)
    first, forward, adjoint = pl.pallas_call(
        stage_kernel,
        out_shape=[
            jax.ShapeDtypeStruct(shape, jnp.bfloat16) for shape in (pair, forward.shape, adjoint.shape)
        ],
        in_specs=[any_space, hbm, any_space, any_space],
        out_specs=[vmem] * 3,
        scratch_shapes=[pltpu.SemaphoreType.DMA((3,))],
        compiler_params=pltpu.CompilerParams(vmem_limit_bytes=16 << 20),
        name="stage_first_pair",
    )(received, dual, forward, adjoint)
    below = facet == facets - 1
    above = facet == 0
    before = jnp.where(above, band > 0, band < bands - 1)
    after = jnp.where(above, band < bands - 1, band > 0)
    flags = [flag.astype(jnp.int32) for flag in (below, above, before, after)]
    info = jnp.stack([own_length[0]] + flags)
    edge_row = jnp.where(above, 0, own_length[0] + ABOVE)
    edges = [lax.dynamic_slice_in_dim(received, h * ext + edge_row, ABOVE, 1) for h in range(2)]
    edges = border_shift(jnp.concatenate(edges, axis=1), bands, facets, 1)
    dual_next, tail, merged, spill, _ = pl.pallas_call(
        functools.partial(facet_kernel, group, ext),
        grid=(subbands // 2,),
        out_shape=(
            pltpu.HBM(dual.shape, jnp.bfloat16),
            jax.ShapeDtypeStruct(pair, jnp.bfloat16),
            jax.ShapeDtypeStruct(received.shape, jnp.float32),
            jax.ShapeDtypeStruct(edges.shape, jnp.float32),
            jax.ShapeDtypeStruct(received.shape, jnp.float32),
        ),
        in_specs=[smem, smem, smem, vmem, vmem, vmem, hbm, vmem, vmem],
        out_specs=(hbm, vmem, vmem, vmem, vmem),
        input_output_aliases={4: 4},
        scratch_shapes=[
            pltpu.VMEM((2,) + pair, jnp.bfloat16),
            pltpu.VMEM((2,) + pair, jnp.bfloat16),
            pltpu.VMEM((2, channels, capacity, columns), jnp.float32),
            pltpu.VMEM((2, capacity, columns), jnp.float32),
            pltpu.VMEM((2, group, capacity + 16, LANES), jnp.float32),
            pltpu.SemaphoreType.DMA((2,)),
            pltpu.SemaphoreType.DMA((2,)),
        ],
        compiler_params=pltpu.CompilerParams(vmem_limit_bytes=36 << 20),
        name="facet_update",
    )(taps.reshape(-1), thresholds, info, edges, received, first, dual, forward, adjoint)

    spill = border_shift(spill, bands, facets, -1)
    dual_next, stored = pl.pallas_call(
        tail_kernel,
        out_shape=(pltpu.HBM(dual.shape, jnp.bfloat16), jax.ShapeDtypeStruct((8, LANES), jnp.float32)),
        in_specs=[vmem, hbm],
        out_specs=(hbm, vmem),
        input_output_aliases={1: 0},
        scratch_shapes=[pltpu.SemaphoreType.DMA],
        compiler_params=pltpu.CompilerParams(vmem_limit_bytes=16 << 20),
        name="store_last_pair",
    )(tail, dual_next)
    merged = pl.pallas_call(
        functools.partial(border_kernel, ext),
        out_shape=jax.ShapeDtypeStruct(received.shape, jnp.float32),
        in_specs=[smem, vmem, vmem, vmem],
        out_specs=vmem,
        input_output_aliases={1: 0},
        compiler_params=pltpu.CompilerParams(vmem_limit_bytes=16 << 20),
        name="add_border_rows",
    )(info, merged, spill, stored)
    returned = lax.all_to_all(merged, "fac", split_axis=0, concat_axis=0, tiled=True)

    prior_term = pl.pallas_call(
        functools.partial(unpack_kernel, capacity, ext),
        out_shape=jax.ShapeDtypeStruct(image_cube.shape, jnp.float32),
        in_specs=[smem, vmem],
        out_specs=hbm,
        scratch_shapes=row_scratch[:2] + [pltpu.SemaphoreType.DMA((6,))],
        compiler_params=pltpu.CompilerParams(vmem_limit_bytes=16 << 20),
        name="unpack_facets",
    )(facet_rows, returned)
    return dual_next, prior_term


def solution(mesh):
    placed = (P("fac", "grp", None), P(None, None, ("grp", "fac"), None), P(), P(), P())
    return jax.shard_map(
        on_device,
        mesh=mesh,
        in_specs=placed,
        out_specs=(P(None, None, ("grp", "fac"), None), P("fac", "grp", None)),
        check_vma=False,
    )
```

```python
import functools

import jax
import jax.numpy as jnp
from jax import lax
from jax.experimental import pallas as pl
from jax.experimental.pallas import tpu as pltpu
from jax.sharding import PartitionSpec as P

TAPS = 4
ABOVE = 2
MARGIN = 8
LANES = 128


def border_shift(x, bands, facets, by):
    pairs = []
    for b in range(bands):
        for facet in range(facets):
            to = b + by if facet % 2 == 0 else b - by
            pairs.append((b * facets + facet, (to % bands) * facets + facet))
    return lax.ppermute(x, ("grp", "fac"), pairs)


def filter_taps(lowpass):
    low = lowpass.astype(jnp.float32)
    parity = jnp.where(jnp.arange(TAPS) % 2 == 0, 1.0, -1.0).astype(jnp.float32)
    return jnp.stack([low, parity * low[:, ::-1]], axis=1)


def column_matrices(taps, columns):
    row = jnp.arange(columns)[:, None]
    col = jnp.arange(columns)[None, :]
    offset = row - col + 2
    total = 0.0
    for k in range(TAPS):
        hit = (offset == k)[None, None]
        total = total + jnp.where(hit, taps[:, :, k, None, None], 0.0)
    return total.astype(jnp.bfloat16)


def facet_starts(rows_ref, starts_ref, facets):
    band = lax.axis_index("grp")

    def step(q, total):
        starts_ref[q] = total
        return total + rows_ref[band, q]

    lax.fori_loop(0, facets, step, jnp.int32(0))


def pack_kernel(per_copy, ext, rows_hbm, image_ref, out_ref, strip, starts, rows_ref, blocks, in_sem, out_sem):
    band_rows = image_ref.shape[1]
    facets = rows_hbm.shape[1]
    steps = facets // per_copy
    fetch_rows = pltpu.make_async_copy(rows_hbm, rows_ref, in_sem.at[2 * steps])
    fetch_rows.start()
    part = band_rows // steps
    copies = [
        [
            pltpu.make_async_copy(
                image_ref.at[0, pl.ds(g * part, part), pl.ds(h * LANES, LANES)],
                strip.at[h, pl.ds(MARGIN + g * part, part)],
                in_sem.at[2 * g + h],
            )
            for h in range(2)
        ]
        for g in range(steps)
    ]
    for pair in copies[-1:] + copies[:-1]:
        for copy in pair:
            copy.start()
    end = MARGIN + band_rows
    for h in range(2):
        strip[h, 0:MARGIN] = jnp.zeros((MARGIN, LANES), jnp.float32)
        strip[h, end:] = jnp.zeros((strip.shape[1] - end, LANES), jnp.float32)
    fetch_rows.wait()
    facet_starts(rows_ref, starts, facets)

    def wait_for(g):
        for copy in copies[g]:
            copy.wait()

    wait_for(steps - 1)
    wait_for(0)
    for h in range(2):
        strip[h, MARGIN - ABOVE : MARGIN] = strip[h, end - ABOVE : end]
        strip[h, end : end + 1] = strip[h, MARGIN : MARGIN + 1]

    arrived = 1
    outs = []
    for g in range(steps):
        while arrived < steps - 1 and arrived * part < (g + 1) * per_copy * (ext - TAPS) + TAPS:
            wait_for(arrived)
            arrived += 1
        for q in range(g * per_copy, (g + 1) * per_copy):
            begin = starts[q] + (MARGIN - ABOVE)
            for h in range(2):
                blocks[q, h * ext : (h + 1) * ext] = strip[h, pl.ds(begin, ext)]
        pick = pl.ds(g * per_copy, per_copy)
        outs.append(pltpu.make_async_copy(blocks.at[pick], out_ref.at[pick], out_sem.at[g]))
        outs[-1].start()
    for copy in outs:
        copy.wait()


def unpack_kernel(capacity, ext, rows_ref, block_ref, out_ref, strip, starts, sem):
    band_rows = out_ref.shape[1]
    facets = block_ref.shape[0]
    end = MARGIN + band_rows
    facet_starts(rows_ref, starts, facets)
    for h in range(2):
        strip[h, 0 : 2 * MARGIN] = jnp.zeros((2 * MARGIN, LANES), jnp.float32)

    copies = []

    def send(begin, stop):
        for h in range(2):
            copies.append(
                pltpu.make_async_copy(
                    strip.at[h, pl.ds(MARGIN + begin, stop - begin)],
                    out_ref.at[0, pl.ds(begin, stop - begin), pl.ds(h * LANES, LANES)],
                    sem.at[len(copies)],
                )
            )
            copies[-1].start()

    shared = lax.broadcasted_iota(jnp.int32, (8, LANES), 0) < 3
    early = 3 * facets // 4
    ready = (band_rows - (facets - early) * capacity) // 8 * 8 - 8
    for q in range(facets):
        if q == early:
            send(8, ready)
        begin = starts[q] + (MARGIN - ABOVE)
        for h in range(2):
            before = strip[h, pl.ds(begin, 8)]
            strip[h, pl.ds(begin, 8)] = block_ref[q, h * ext : h * ext + 8] + jnp.where(shared, before, 0.0)
            strip[h, pl.ds(begin + 8, ext - 8)] = block_ref[q, h * ext + 8 : (h + 1) * ext]
    for h in range(2):
        strip[h, end - ABOVE : end] += strip[h, MARGIN - ABOVE : MARGIN]
        strip[h, MARGIN : MARGIN + 1] += strip[h, end : end + 1]
    send(0, 8)
    send(ready, band_rows)
    for copy in copies:
        copy.wait()


def stage_kernel(received_ref, dual_hbm, fwd_any, adj_any, first_ref, fwd_ref, adj_ref, sem):
    pairs = ((dual_hbm.at[pl.ds(0, 2)], first_ref), (fwd_any, fwd_ref), (adj_any, adj_ref))
    copies = [pltpu.make_async_copy(src, dst, sem.at[i]) for i, (src, dst) in enumerate(pairs)]
    for copy in copies:
        copy.start()
    for copy in copies:
        copy.wait()


def tail_kernel(tail_ref, begun_hbm, next_hbm, done_ref, sem):
    pair = tail_ref.shape[0]
    copy = pltpu.make_async_copy(tail_ref, next_hbm.at[pl.ds(next_hbm.shape[0] - pair, pair)], sem)
    copy.start()
    done_ref[...] = jnp.zeros_like(done_ref)
    copy.wait()


def facet_kernel(group, ext, taps_ref, thr_ref, info_ref, edge_ref, received_ref, first_ref, dual_hbm, fwd_ref, adj_ref,
                 next_hbm, tail_ref, merged_ref, spill_ref, x_ref,
                 in_slots, out_slots, u_ref, sq_ref, z_ref, in_sem, out_sem):
    steps = dual_hbm.shape[0] // 2
    channels, capacity, columns = dual_hbm.shape[1:]
    rows = group * capacity
    length, below, above = info_ref[0], info_ref[1], info_ref[2]
    inside = info_ref[3].astype(jnp.float32)
    spans = [(1, 3) if step < steps // 2 else (0, TAPS) for step in range(steps)]
    sources = [first_ref] + [in_slots.at[step % 2] for step in range(1, steps)]
    targets = [out_slots.at[step % 2] for step in range(steps - 1)] + [tail_ref]
    fetches = [
        pltpu.make_async_copy(dual_hbm.at[pl.ds(2 * step, 2)], in_slots.at[step % 2], in_sem.at[step % 2])
        for step in range(steps)
    ]
    stores = [
        pltpu.make_async_copy(out_slots.at[step % 2], next_hbm.at[pl.ds(2 * step, 2)], out_sem.at[step % 2])
        for step in range(steps)
    ]
    for step in range(1, 3):
        fetches[step].start()
    z_ref[...] = jnp.zeros_like(z_ref)

    @pl.when(above == 1)
    def _():
        for h in range(2):
            x_ref[:, h * ext : h * ext + ABOVE, :] = inside * edge_ref[:, ABOVE * h : ABOVE * (h + 1), :]

    @pl.when(below == 1)
    def _():
        for h in range(2):
            row = pl.ds(h * ext + ABOVE + length, 1)
            x_ref[:, row, :] = inside * edge_ref[:, ABOVE * h : ABOVE * h + 1, :]

    def analyse(step, i):
        pick = pl.ds(i * group, group)
        begin, stop = spans[step]
        taps = [taps_ref[step * TAPS + k] for k in range(TAPS)]
        halves = []
        for h in range(2):
            total = taps[begin] * x_ref[pick, h * ext + begin : h * ext + begin + capacity, :]
            for k in range(begin + 1, stop):
                total = total + taps[k] * x_ref[pick, h * ext + k : h * ext + k + capacity, :]
            halves.append(total.reshape(rows, LANES))
        filtered = jnp.concatenate(halves, axis=1)
        high = filtered.astype(jnp.bfloat16)
        low = (filtered - high.astype(jnp.float32)).astype(jnp.bfloat16)
        coefficient = jnp.dot(
            jnp.concatenate([high, low], axis=1), fwd_ref[step // 2], preferred_element_type=jnp.float32
        )
        for b in range(2):
            part = coefficient[:, b * columns : (b + 1) * columns].reshape(group, capacity, columns)
            combined = part + sources[step][b, pick].astype(jnp.float32)
            u_ref[step % 2, b, pick] = combined
            sq_ref[step % 2, b] += jnp.sum(combined * combined, axis=0)

    def synthesise(step, i):
        pick = pl.ds(i * group, group)
        begin, stop = spans[step]
        taps = [taps_ref[step * TAPS + k] for k in range(TAPS)]
        parts = []
        for b in range(2):
            scaled = u_ref[step % 2, b, pick] * sq_ref[step % 2, b][None]
            targets[step][b, pick] = scaled.astype(jnp.bfloat16)
            parts.append(scaled.reshape(rows, columns).astype(jnp.bfloat16))
        z = jnp.dot(jnp.concatenate(parts, axis=1), adj_ref[step // 2], preferred_element_type=jnp.float32)
        z = z.reshape(group, capacity, columns)
        for h in range(2):
            z_ref[h, :, 8 : 8 + capacity, :] = z[:, :, h * LANES : (h + 1) * LANES]
        for h in range(2):
            total = taps[begin] * z_ref[h, :, 8 - begin : 8 - begin + ext, :]
            for k in range(begin + 1, stop):
                total = total + taps[k] * z_ref[h, :, 8 - k : 8 - k + ext, :]
            if step == 0:
                merged_ref[pick, h * ext : (h + 1) * ext, :] = total
            else:
                merged_ref[pick, h * ext : (h + 1) * ext, :] += total

    keep = lax.broadcasted_iota(jnp.int32, (capacity, columns), 0) < length
    for stage in range(steps + 1):
        if 0 < stage < steps:
            fetches[stage].wait()
        if stage == 3:
            stores[0].wait()
        if stage < steps:
            sq_ref[stage % 2] = jnp.zeros_like(sq_ref[stage % 2])

        def work(i):
            if stage > 0:
                synthesise(stage - 1, i)
            if stage < steps:
                analyse(stage, i)

        if stage > 0:
            pl.loop(0, channels // group)(lambda i: synthesise(stage - 1, i))
        if stage < steps:
            pl.loop(0, channels // group)(lambda i: analyse(stage, i))
        if stage == 1:
            fetches[3].start()
        if 0 < stage < steps:
            stores[stage - 1].start()
        if stage < steps:
            for b in range(2):
                radius = thr_ref[stage * 2 + b]
                scale = radius / jnp.maximum(jnp.sqrt(sq_ref[stage % 2, b]), radius)
                sq_ref[stage % 2, b] = jnp.where(keep, scale, 0.0)

    spill_ref[...] = jnp.zeros_like(spill_ref)

    @pl.when(above == 1)
    def _():
        for h in range(2):
            spill_ref[:, ABOVE * h : ABOVE * (h + 1), :] = merged_ref[:, h * ext : h * ext + ABOVE, :]

    @pl.when(below == 1)
    def _():
        for h in range(2):
            row = pl.ds(h * ext + ABOVE + length, 1)
            spill_ref[:, ABOVE * h : ABOVE * h + 1, :] = merged_ref[:, row, :]

    stores[1].wait()
    stores[2].wait()


def border_kernel(ext, info_ref, sent_ref, spill_ref, stored_ref, merged_ref):
    length, below, above = info_ref[0], info_ref[1], info_ref[2]
    inside = info_ref[4].astype(jnp.float32)

    @pl.when(above == 1)
    def _():
        for h in range(2):
            merged_ref[:, h * ext : h * ext + ABOVE, :] = inside * spill_ref[:, ABOVE * h : ABOVE * (h + 1), :]

    @pl.when(below == 1)
    def _():
        for h in range(2):
            row = pl.ds(h * ext + ABOVE + length, 1)
            merged_ref[:, row, :] = inside * spill_ref[:, ABOVE * h : ABOVE * h + 1, :]


def on_device(image_cube, dual, lowpass, thresholds, facet_rows):
    band = lax.axis_index("grp")
    facet = lax.axis_index("fac")
    facets = lax.axis_size("fac")
    bands = lax.axis_size("grp")
    _, band_rows, columns = image_cube.shape
    subbands, channels, capacity, _ = dual.shape
    ext = capacity + TAPS
    per_step = 4
    strip_rows = MARGIN + band_rows + capacity
    lengths = lax.dynamic_index_in_dim(facet_rows, band, 0, keepdims=False)
    own_length = lax.dynamic_slice_in_dim(lengths, facet, 1)

    row_scratch = [
        pltpu.VMEM((2, strip_rows, LANES), jnp.float32),
        pltpu.SMEM((facets,), jnp.int32),
    ]
    smem = pl.BlockSpec(memory_space=pltpu.SMEM)
    vmem = pl.BlockSpec(memory_space=pltpu.VMEM)
    hbm = pl.BlockSpec(memory_space=pltpu.HBM)
    packed = pl.pallas_call(
        functools.partial(pack_kernel, per_step, ext),
        out_shape=pltpu.HBM((facets, 2 * ext, LANES), jnp.float32),
        in_specs=[hbm, hbm],
        out_specs=hbm,
        scratch_shapes=row_scratch[:2] + [
            pltpu.SMEM(facet_rows.shape, jnp.int32),
            pltpu.VMEM((facets, 2 * ext, LANES), jnp.float32),
            pltpu.SemaphoreType.DMA((2 * (facets // per_step) + 1,)),
            pltpu.SemaphoreType.DMA((facets // per_step,)),
        ],
        compiler_params=pltpu.CompilerParams(vmem_limit_bytes=16 << 20),
        name="pack_facets",
    )(*(pltpu.with_memory_space_constraint(a, pltpu.HBM) for a in (facet_rows, image_cube)))

    received = lax.all_to_all(packed, "fac", split_axis=0, concat_axis=0, tiled=True)

    taps = filter_taps(lowpass)
    matrices = column_matrices(taps, columns)
    forward = jnp.concatenate([matrices[:, 0], matrices[:, 1]], axis=2)
    forward = jnp.concatenate([forward, forward], axis=1)
    swapped = jnp.swapaxes(matrices, 2, 3)
    adjoint = jnp.concatenate([swapped[:, 0], swapped[:, 1]], axis=1)
    group = 16
    dual = pltpu.with_memory_space_constraint(dual, pltpu.HBM)
    pair = (2,) + dual.shape[1:]
    any_space = pl.BlockSpec(memory_space=pl.ANY)
    first, forward, adjoint = pl.pallas_call(
        stage_kernel,
        out_shape=[
            jax.ShapeDtypeStruct(shape, jnp.bfloat16) for shape in (pair, forward.shape, adjoint.shape)
        ],
        in_specs=[any_space, hbm, any_space, any_space],
        out_specs=[vmem] * 3,
        scratch_shapes=[pltpu.SemaphoreType.DMA((3,))],
        compiler_params=pltpu.CompilerParams(vmem_limit_bytes=16 << 20),
        name="stage_first_pair",
    )(received, dual, forward, adjoint)
    below = facet == facets - 1
    above = facet == 0
    before = jnp.where(above, band > 0, band < bands - 1)
    after = jnp.where(above, band < bands - 1, band > 0)
    flags = [flag.astype(jnp.int32) for flag in (below, above, before, after)]
    info = jnp.stack([own_length[0]] + flags)
    edge_row = jnp.where(above, 0, own_length[0] + ABOVE)
    edges = [lax.dynamic_slice_in_dim(received, h * ext + edge_row, ABOVE, 1) for h in range(2)]
    edges = border_shift(jnp.concatenate(edges, axis=1), bands, facets, 1)
    dual_next, tail, merged, spill, _ = pl.pallas_call(
        functools.partial(facet_kernel, group, ext),
        out_shape=(
            pltpu.HBM(dual.shape, jnp.bfloat16),
            jax.ShapeDtypeStruct(pair, jnp.bfloat16),
            jax.ShapeDtypeStruct(received.shape, jnp.float32),
            jax.ShapeDtypeStruct(edges.shape, jnp.float32),
            jax.ShapeDtypeStruct(received.shape, jnp.float32),
        ),
        in_specs=[smem, smem, smem, vmem, vmem, vmem, hbm, vmem, vmem],
        out_specs=(hbm, vmem, vmem, vmem, vmem),
        input_output_aliases={4: 4},
        scratch_shapes=[
            pltpu.VMEM((2,) + pair, jnp.bfloat16),
            pltpu.VMEM((2,) + pair, jnp.bfloat16),
            pltpu.VMEM((2, 2, channels, capacity, columns), jnp.float32),
            pltpu.VMEM((2, 2, capacity, columns), jnp.float32),
            pltpu.VMEM((2, group, capacity + 16, LANES), jnp.float32),
            pltpu.SemaphoreType.DMA((2,)),
            pltpu.SemaphoreType.DMA((2,)),
        ],
        compiler_params=pltpu.CompilerParams(vmem_limit_bytes=36 << 20),
        name="facet_update",
    )(taps.reshape(-1), thresholds, info, edges, received, first, dual, forward, adjoint)

    spill = border_shift(spill, bands, facets, -1)
    dual_next, stored = pl.pallas_call(
        tail_kernel,
        out_shape=(pltpu.HBM(dual.shape, jnp.bfloat16), jax.ShapeDtypeStruct((8, LANES), jnp.float32)),
        in_specs=[vmem, hbm],
        out_specs=(hbm, vmem),
        input_output_aliases={1: 0},
        scratch_shapes=[pltpu.SemaphoreType.DMA],
        compiler_params=pltpu.CompilerParams(vmem_limit_bytes=16 << 20),
        name="store_last_pair",
    )(tail, dual_next)
    merged = pl.pallas_call(
        functools.partial(border_kernel, ext),
        out_shape=jax.ShapeDtypeStruct(received.shape, jnp.float32),
        in_specs=[smem, vmem, vmem, vmem],
        out_specs=vmem,
        input_output_aliases={1: 0},
        compiler_params=pltpu.CompilerParams(vmem_limit_bytes=16 << 20),
        name="add_border_rows",
    )(info, merged, spill, stored)
    returned = lax.all_to_all(merged, "fac", split_axis=0, concat_axis=0, tiled=True)

    prior_term = pl.pallas_call(
        functools.partial(unpack_kernel, capacity, ext),
        out_shape=jax.ShapeDtypeStruct(image_cube.shape, jnp.float32),
        in_specs=[smem, vmem],
        out_specs=hbm,
        scratch_shapes=row_scratch[:2] + [pltpu.SemaphoreType.DMA((6,))],
        compiler_params=pltpu.CompilerParams(vmem_limit_bytes=16 << 20),
        name="unpack_facets",
    )(facet_rows, returned)
    return dual_next, prior_term


def solution(mesh):
    placed = (P("fac", "grp", None), P(None, None, ("grp", "fac"), None), P(), P(), P())
    return jax.shard_map(
        on_device,
        mesh=mesh,
        in_specs=placed,
        out_specs=(P(None, None, ("grp", "fac"), None), P("fac", "grp", None)),
        check_vma=False,
    )
```

```python
import functools

import jax
import jax.numpy as jnp
from jax import lax
from jax.experimental import pallas as pl
from jax.experimental.pallas import tpu as pltpu
from jax.sharding import PartitionSpec as P

TAPS = 4
ABOVE = 2
MARGIN = 8
LANES = 128


def border_shift(x, bands, facets, by):
    pairs = []
    for b in range(bands):
        for facet in range(facets):
            to = b + by if facet % 2 == 0 else b - by
            pairs.append((b * facets + facet, (to % bands) * facets + facet))
    return lax.ppermute(x, ("grp", "fac"), pairs)


def filter_taps(lowpass):
    low = lowpass.astype(jnp.float32)
    parity = jnp.where(jnp.arange(TAPS) % 2 == 0, 1.0, -1.0).astype(jnp.float32)
    return jnp.stack([low, parity * low[:, ::-1]], axis=1)


def column_matrices(taps, columns):
    row = jnp.arange(columns)[:, None]
    col = jnp.arange(columns)[None, :]
    offset = row - col + 2
    total = 0.0
    for k in range(TAPS):
        hit = (offset == k)[None, None]
        total = total + jnp.where(hit, taps[:, :, k, None, None], 0.0)
    return total.astype(jnp.bfloat16)


def facet_starts(rows_ref, starts_ref, facets):
    band = lax.axis_index("grp")

    def step(q, total):
        starts_ref[q] = total
        return total + rows_ref[band, q]

    lax.fori_loop(0, facets, step, jnp.int32(0))


def pack_kernel(per_copy, ext, rows_hbm, image_ref, out_ref, strip, starts, rows_ref, blocks, in_sem, out_sem):
    band_rows = image_ref.shape[1]
    facets = rows_hbm.shape[1]
    steps = facets // per_copy
    fetch_rows = pltpu.make_async_copy(rows_hbm, rows_ref, in_sem.at[2 * steps])
    fetch_rows.start()
    part = band_rows // steps
    copies = [
        [
            pltpu.make_async_copy(
                image_ref.at[0, pl.ds(g * part, part), pl.ds(h * LANES, LANES)],
                strip.at[h, pl.ds(MARGIN + g * part, part)],
                in_sem.at[2 * g + h],
            )
            for h in range(2)
        ]
        for g in range(steps)
    ]
    for pair in copies[-1:] + copies[:-1]:
        for copy in pair:
            copy.start()
    end = MARGIN + band_rows
    for h in range(2):
        strip[h, 0:MARGIN] = jnp.zeros((MARGIN, LANES), jnp.float32)
        strip[h, end:] = jnp.zeros((strip.shape[1] - end, LANES), jnp.float32)
    fetch_rows.wait()
    facet_starts(rows_ref, starts, facets)

    def wait_for(g):
        for copy in copies[g]:
            copy.wait()

    wait_for(steps - 1)
    wait_for(0)
    for h in range(2):
        strip[h, MARGIN - ABOVE : MARGIN] = strip[h, end - ABOVE : end]
        strip[h, end : end + 1] = strip[h, MARGIN : MARGIN + 1]

    arrived = 1
    outs = []
    for g in range(steps):
        while arrived < steps - 1 and arrived * part < (g + 1) * per_copy * (ext - TAPS) + TAPS:
            wait_for(arrived)
            arrived += 1
        for q in range(g * per_copy, (g + 1) * per_copy):
            begin = starts[q] + (MARGIN - ABOVE)
            for h in range(2):
                blocks[q, h * ext : (h + 1) * ext] = strip[h, pl.ds(begin, ext)]
        pick = pl.ds(g * per_copy, per_copy)
        outs.append(pltpu.make_async_copy(blocks.at[pick], out_ref.at[pick], out_sem.at[g]))
        outs[-1].start()
    for copy in outs:
        copy.wait()


def unpack_kernel(capacity, ext, rows_ref, block_ref, out_ref, strip, starts, sem):
    band_rows = out_ref.shape[1]
    facets = block_ref.shape[0]
    end = MARGIN + band_rows
    facet_starts(rows_ref, starts, facets)
    for h in range(2):
        strip[h, 0 : 2 * MARGIN] = jnp.zeros((2 * MARGIN, LANES), jnp.float32)

    copies = []

    def send(begin, stop):
        for h in range(2):
            copies.append(
                pltpu.make_async_copy(
                    strip.at[h, pl.ds(MARGIN + begin, stop - begin)],
                    out_ref.at[0, pl.ds(begin, stop - begin), pl.ds(h * LANES, LANES)],
                    sem.at[len(copies)],
                )
            )
            copies[-1].start()

    shared = lax.broadcasted_iota(jnp.int32, (8, LANES), 0) < 3
    sent = 8
    early = (facets // 2, 3 * facets // 4, 7 * facets // 8, 15 * facets // 16)
    for q in range(facets):
        if q in early:
            ready = (band_rows - (facets - q) * capacity) // 8 * 8 - 8
            send(sent, ready)
            sent = ready
        begin = starts[q] + (MARGIN - ABOVE)
        for h in range(2):
            before = strip[h, pl.ds(begin, 8)]
            strip[h, pl.ds(begin, 8)] = block_ref[q, h * ext : h * ext + 8] + jnp.where(shared, before, 0.0)
            strip[h, pl.ds(begin + 8, ext - 8)] = block_ref[q, h * ext + 8 : (h + 1) * ext]
    for h in range(2):
        strip[h, end - ABOVE : end] += strip[h, MARGIN - ABOVE : MARGIN]
        strip[h, MARGIN : MARGIN + 1] += strip[h, end : end + 1]
    send(0, 8)
    send(sent, band_rows)
    for copy in copies:
        copy.wait()


def stage_kernel(received_ref, dual_hbm, fwd_any, adj_any, first_ref, fwd_ref, adj_ref, sem):
    pairs = ((dual_hbm.at[pl.ds(0, 2)], first_ref), (fwd_any, fwd_ref), (adj_any, adj_ref))
    copies = [pltpu.make_async_copy(src, dst, sem.at[i]) for i, (src, dst) in enumerate(pairs)]
    for copy in copies:
        copy.start()
    for copy in copies:
        copy.wait()


def tail_kernel(tail_ref, begun_hbm, next_hbm, done_ref, sem):
    pair = tail_ref.shape[0]
    copy = pltpu.make_async_copy(tail_ref, next_hbm.at[pl.ds(next_hbm.shape[0] - pair, pair)], sem)
    copy.start()
    done_ref[...] = jnp.zeros_like(done_ref)
    copy.wait()


def facet_kernel(group, ext, taps_ref, thr_ref, info_ref, edge_ref, received_ref, first_ref, dual_hbm, fwd_ref, adj_ref,
                 next_hbm, tail_ref, merged_ref, spill_ref, x_ref,
                 in_slots, out_slots, u_ref, sq_ref, z_ref, in_sem, out_sem):
    steps = dual_hbm.shape[0] // 2
    channels, capacity, columns = dual_hbm.shape[1:]
    rows = group * capacity
    length, below, above = info_ref[0], info_ref[1], info_ref[2]
    inside = info_ref[3].astype(jnp.float32)
    spans = [(1, 3) if step < steps // 2 else (0, TAPS) for step in range(steps)]
    sources = [first_ref] + [in_slots.at[step % 2] for step in range(1, steps)]
    targets = [out_slots.at[step % 2] for step in range(steps - 1)] + [tail_ref]
    fetches = [
        pltpu.make_async_copy(dual_hbm.at[pl.ds(2 * step, 2)], in_slots.at[step % 2], in_sem.at[step % 2])
        for step in range(steps)
    ]
    stores = [
        pltpu.make_async_copy(out_slots.at[step % 2], next_hbm.at[pl.ds(2 * step, 2)], out_sem.at[step % 2])
        for step in range(steps)
    ]
    for step in range(1, 3):
        fetches[step].start()
    z_ref[...] = jnp.zeros_like(z_ref)

    @pl.when(above == 1)
    def _():
        for h in range(2):
            x_ref[:, h * ext : h * ext + ABOVE, :] = inside * edge_ref[:, ABOVE * h : ABOVE * (h + 1), :]

    @pl.when(below == 1)
    def _():
        for h in range(2):
            row = pl.ds(h * ext + ABOVE + length, 1)
            x_ref[:, row, :] = inside * edge_ref[:, ABOVE * h : ABOVE * h + 1, :]

    def analyse(step, i):
        pick = pl.ds(i * group, group)
        begin, stop = spans[step]
        taps = [taps_ref[step * TAPS + k] for k in range(TAPS)]
        halves = []
        for h in range(2):
            total = taps[begin] * x_ref[pick, h * ext + begin : h * ext + begin + capacity, :]
            for k in range(begin + 1, stop):
                total = total + taps[k] * x_ref[pick, h * ext + k : h * ext + k + capacity, :]
            halves.append(total.reshape(rows, LANES))
        filtered = jnp.concatenate(halves, axis=1)
        high = filtered.astype(jnp.bfloat16)
        low = (filtered - high.astype(jnp.float32)).astype(jnp.bfloat16)
        coefficient = jnp.dot(
            jnp.concatenate([high, low], axis=1), fwd_ref[step // 2], preferred_element_type=jnp.float32
        )
        for b in range(2):
            part = coefficient[:, b * columns : (b + 1) * columns].reshape(group, capacity, columns)
            combined = part + sources[step][b, pick].astype(jnp.float32)
            u_ref[step % 2, b, pick] = combined
            sq_ref[step % 2, b] += jnp.sum(combined * combined, axis=0)

    def synthesise(step, i):
        pick = pl.ds(i * group, group)
        begin, stop = spans[step]
        taps = [taps_ref[step * TAPS + k] for k in range(TAPS)]
        parts = []
        for b in range(2):
            scaled = u_ref[step % 2, b, pick] * sq_ref[step % 2, b][None]
            targets[step][b, pick] = scaled.astype(jnp.bfloat16)
            parts.append(scaled.reshape(rows, columns).astype(jnp.bfloat16))
        z = jnp.dot(jnp.concatenate(parts, axis=1), adj_ref[step // 2], preferred_element_type=jnp.float32)
        z = z.reshape(group, capacity, columns)
        for h in range(2):
            z_ref[h, :, 8 : 8 + capacity, :] = z[:, :, h * LANES : (h + 1) * LANES]
        for h in range(2):
            total = taps[begin] * z_ref[h, :, 8 - begin : 8 - begin + ext, :]
            for k in range(begin + 1, stop):
                total = total + taps[k] * z_ref[h, :, 8 - k : 8 - k + ext, :]
            if step == 0:
                merged_ref[pick, h * ext : (h + 1) * ext, :] = total
            else:
                merged_ref[pick, h * ext : (h + 1) * ext, :] += total

    keep = lax.broadcasted_iota(jnp.int32, (capacity, columns), 0) < length
    for stage in range(steps + 1):
        if 0 < stage < steps:
            fetches[stage].wait()
        if stage == 3:
            stores[0].wait()
        if stage < steps:
            sq_ref[stage % 2] = jnp.zeros_like(sq_ref[stage % 2])

        def work(i):
            if stage > 0:
                synthesise(stage - 1, i)
            if stage < steps:
                analyse(stage, i)

        if stage > 0:
            pl.loop(0, channels // group)(lambda i: synthesise(stage - 1, i))
        if stage < steps:
            pl.loop(0, channels // group)(lambda i: analyse(stage, i))
        if stage == 1:
            fetches[3].start()
        if 0 < stage < steps:
            stores[stage - 1].start()
        if stage < steps:
            for b in range(2):
                radius = thr_ref[stage * 2 + b]
                scale = radius / jnp.maximum(jnp.sqrt(sq_ref[stage % 2, b]), radius)
                sq_ref[stage % 2, b] = jnp.where(keep, scale, 0.0)

    spill_ref[...] = jnp.zeros_like(spill_ref)

    @pl.when(above == 1)
    def _():
        for h in range(2):
            spill_ref[:, ABOVE * h : ABOVE * (h + 1), :] = merged_ref[:, h * ext : h * ext + ABOVE, :]

    @pl.when(below == 1)
    def _():
        for h in range(2):
            row = pl.ds(h * ext + ABOVE + length, 1)
            spill_ref[:, ABOVE * h : ABOVE * h + 1, :] = merged_ref[:, row, :]

    stores[1].wait()
    stores[2].wait()


def border_kernel(ext, info_ref, sent_ref, spill_ref, stored_ref, merged_ref):
    length, below, above = info_ref[0], info_ref[1], info_ref[2]
    inside = info_ref[4].astype(jnp.float32)

    @pl.when(above == 1)
    def _():
        for h in range(2):
            merged_ref[:, h * ext : h * ext + ABOVE, :] = inside * spill_ref[:, ABOVE * h : ABOVE * (h + 1), :]

    @pl.when(below == 1)
    def _():
        for h in range(2):
            row = pl.ds(h * ext + ABOVE + length, 1)
            merged_ref[:, row, :] = inside * spill_ref[:, ABOVE * h : ABOVE * h + 1, :]


def on_device(image_cube, dual, lowpass, thresholds, facet_rows):
    band = lax.axis_index("grp")
    facet = lax.axis_index("fac")
    facets = lax.axis_size("fac")
    bands = lax.axis_size("grp")
    _, band_rows, columns = image_cube.shape
    subbands, channels, capacity, _ = dual.shape
    ext = capacity + TAPS
    per_step = 4
    strip_rows = MARGIN + band_rows + capacity
    lengths = lax.dynamic_index_in_dim(facet_rows, band, 0, keepdims=False)
    own_length = lax.dynamic_slice_in_dim(lengths, facet, 1)

    row_scratch = [
        pltpu.VMEM((2, strip_rows, LANES), jnp.float32),
        pltpu.SMEM((facets,), jnp.int32),
    ]
    smem = pl.BlockSpec(memory_space=pltpu.SMEM)
    vmem = pl.BlockSpec(memory_space=pltpu.VMEM)
    hbm = pl.BlockSpec(memory_space=pltpu.HBM)
    packed = pl.pallas_call(
        functools.partial(pack_kernel, per_step, ext),
        out_shape=pltpu.HBM((facets, 2 * ext, LANES), jnp.float32),
        in_specs=[hbm, hbm],
        out_specs=hbm,
        scratch_shapes=row_scratch[:2] + [
            pltpu.SMEM(facet_rows.shape, jnp.int32),
            pltpu.VMEM((facets, 2 * ext, LANES), jnp.float32),
            pltpu.SemaphoreType.DMA((2 * (facets // per_step) + 1,)),
            pltpu.SemaphoreType.DMA((facets // per_step,)),
        ],
        compiler_params=pltpu.CompilerParams(vmem_limit_bytes=16 << 20),
        name="pack_facets",
    )(*(pltpu.with_memory_space_constraint(a, pltpu.HBM) for a in (facet_rows, image_cube)))

    received = lax.all_to_all(packed, "fac", split_axis=0, concat_axis=0, tiled=True)

    taps = filter_taps(lowpass)
    matrices = column_matrices(taps, columns)
    forward = jnp.concatenate([matrices[:, 0], matrices[:, 1]], axis=2)
    forward = jnp.concatenate([forward, forward], axis=1)
    swapped = jnp.swapaxes(matrices, 2, 3)
    adjoint = jnp.concatenate([swapped[:, 0], swapped[:, 1]], axis=1)
    group = 16
    dual = pltpu.with_memory_space_constraint(dual, pltpu.HBM)
    pair = (2,) + dual.shape[1:]
    any_space = pl.BlockSpec(memory_space=pl.ANY)
    first, forward, adjoint = pl.pallas_call(
        stage_kernel,
        out_shape=[
            jax.ShapeDtypeStruct(shape, jnp.bfloat16) for shape in (pair, forward.shape, adjoint.shape)
        ],
        in_specs=[any_space, hbm, any_space, any_space],
        out_specs=[vmem] * 3,
        scratch_shapes=[pltpu.SemaphoreType.DMA((3,))],
        compiler_params=pltpu.CompilerParams(vmem_limit_bytes=16 << 20),
        name="stage_first_pair",
    )(received, dual, forward, adjoint)
    below = facet == facets - 1
    above = facet == 0
    before = jnp.where(above, band > 0, band < bands - 1)
    after = jnp.where(above, band < bands - 1, band > 0)
    flags = [flag.astype(jnp.int32) for flag in (below, above, before, after)]
    info = jnp.stack([own_length[0]] + flags)
    edge_row = jnp.where(above, 0, own_length[0] + ABOVE)
    edges = [lax.dynamic_slice_in_dim(received, h * ext + edge_row, ABOVE, 1) for h in range(2)]
    edges = border_shift(jnp.concatenate(edges, axis=1), bands, facets, 1)
    dual_next, tail, merged, spill, _ = pl.pallas_call(
        functools.partial(facet_kernel, group, ext),
        out_shape=(
            pltpu.HBM(dual.shape, jnp.bfloat16),
            jax.ShapeDtypeStruct(pair, jnp.bfloat16),
            jax.ShapeDtypeStruct(received.shape, jnp.float32),
            jax.ShapeDtypeStruct(edges.shape, jnp.float32),
            jax.ShapeDtypeStruct(received.shape, jnp.float32),
        ),
        in_specs=[smem, smem, smem, vmem, vmem, vmem, hbm, vmem, vmem],
        out_specs=(hbm, vmem, vmem, vmem, vmem),
        input_output_aliases={4: 4},
        scratch_shapes=[
            pltpu.VMEM((2,) + pair, jnp.bfloat16),
            pltpu.VMEM((2,) + pair, jnp.bfloat16),
            pltpu.VMEM((2, 2, channels, capacity, columns), jnp.float32),
            pltpu.VMEM((2, 2, capacity, columns), jnp.float32),
            pltpu.VMEM((2, group, capacity + 16, LANES), jnp.float32),
            pltpu.SemaphoreType.DMA((2,)),
            pltpu.SemaphoreType.DMA((2,)),
        ],
        compiler_params=pltpu.CompilerParams(vmem_limit_bytes=36 << 20),
        name="facet_update",
    )(taps.reshape(-1), thresholds, info, edges, received, first, dual, forward, adjoint)

    spill = border_shift(spill, bands, facets, -1)
    dual_next, stored = pl.pallas_call(
        tail_kernel,
        out_shape=(pltpu.HBM(dual.shape, jnp.bfloat16), jax.ShapeDtypeStruct((8, LANES), jnp.float32)),
        in_specs=[vmem, hbm],
        out_specs=(hbm, vmem),
        input_output_aliases={1: 0},
        scratch_shapes=[pltpu.SemaphoreType.DMA],
        compiler_params=pltpu.CompilerParams(vmem_limit_bytes=16 << 20),
        name="store_last_pair",
    )(tail, dual_next)
    merged = pl.pallas_call(
        functools.partial(border_kernel, ext),
        out_shape=jax.ShapeDtypeStruct(received.shape, jnp.float32),
        in_specs=[smem, vmem, vmem, vmem],
        out_specs=vmem,
        input_output_aliases={1: 0},
        compiler_params=pltpu.CompilerParams(vmem_limit_bytes=16 << 20),
        name="add_border_rows",
    )(info, merged, spill, stored)
    returned = lax.all_to_all(merged, "fac", split_axis=0, concat_axis=0, tiled=True)

    prior_term = pl.pallas_call(
        functools.partial(unpack_kernel, capacity, ext),
        out_shape=jax.ShapeDtypeStruct(image_cube.shape, jnp.float32),
        in_specs=[smem, vmem],
        out_specs=hbm,
        scratch_shapes=row_scratch[:2] + [pltpu.SemaphoreType.DMA((12,))],
        compiler_params=pltpu.CompilerParams(vmem_limit_bytes=16 << 20),
        name="unpack_facets",
    )(facet_rows, returned)
    return dual_next, prior_term


def solution(mesh):
    placed = (P("fac", "grp", None), P(None, None, ("grp", "fac"), None), P(), P(), P())
    return jax.shard_map(
        on_device,
        mesh=mesh,
        in_specs=placed,
        out_specs=(P(None, None, ("grp", "fac"), None), P("fac", "grp", None)),
        check_vma=False,
    )
```

```python
import functools

import jax
import jax.numpy as jnp
from jax import lax
from jax.experimental import pallas as pl
from jax.experimental.pallas import tpu as pltpu
from jax.sharding import PartitionSpec as P

TAPS = 4
ABOVE = 2
MARGIN = 8
LANES = 128


def border_shift(x, bands, facets, by):
    pairs = []
    for b in range(bands):
        for facet in range(facets):
            to = b + by if facet % 2 == 0 else b - by
            pairs.append((b * facets + facet, (to % bands) * facets + facet))
    return lax.ppermute(x, ("grp", "fac"), pairs)


def filter_taps(lowpass):
    low = lowpass.astype(jnp.float32)
    parity = jnp.where(jnp.arange(TAPS) % 2 == 0, 1.0, -1.0).astype(jnp.float32)
    return jnp.stack([low, parity * low[:, ::-1]], axis=1)


def column_matrices(taps, columns):
    row = jnp.arange(columns)[:, None]
    col = jnp.arange(columns)[None, :]
    offset = row - col + 2
    total = 0.0
    for k in range(TAPS):
        hit = (offset == k)[None, None]
        total = total + jnp.where(hit, taps[:, :, k, None, None], 0.0)
    return total.astype(jnp.bfloat16)


def facet_starts(rows_ref, starts_ref, facets):
    band = lax.axis_index("grp")

    def step(q, total):
        starts_ref[q] = total
        return total + rows_ref[band, q]

    lax.fori_loop(0, facets, step, jnp.int32(0))


def pack_kernel(per_copy, ext, rows_hbm, image_ref, out_ref, strip, starts, rows_ref, blocks, in_sem, out_sem):
    band_rows = image_ref.shape[1]
    facets = rows_hbm.shape[1]
    steps = facets // per_copy
    fetch_rows = pltpu.make_async_copy(rows_hbm, rows_ref, in_sem.at[2 * steps])
    fetch_rows.start()
    part = band_rows // steps
    copies = [
        [
            pltpu.make_async_copy(
                image_ref.at[0, pl.ds(g * part, part), pl.ds(h * LANES, LANES)],
                strip.at[h, pl.ds(MARGIN + g * part, part)],
                in_sem.at[2 * g + h],
            )
            for h in range(2)
        ]
        for g in range(steps)
    ]
    for pair in copies[-1:] + copies[:-1]:
        for copy in pair:
            copy.start()
    end = MARGIN + band_rows
    for h in range(2):
        strip[h, 0:MARGIN] = jnp.zeros((MARGIN, LANES), jnp.float32)
        strip[h, end:] = jnp.zeros((strip.shape[1] - end, LANES), jnp.float32)
    fetch_rows.wait()
    facet_starts(rows_ref, starts, facets)

    def wait_for(g):
        for copy in copies[g]:
            copy.wait()

    wait_for(steps - 1)
    wait_for(0)
    for h in range(2):
        strip[h, MARGIN - ABOVE : MARGIN] = strip[h, end - ABOVE : end]
        strip[h, end : end + 1] = strip[h, MARGIN : MARGIN + 1]

    arrived = 1
    outs = []
    for g in range(steps):
        while arrived < steps - 1 and arrived * part < (g + 1) * per_copy * (ext - TAPS) + TAPS:
            wait_for(arrived)
            arrived += 1
        for q in range(g * per_copy, (g + 1) * per_copy):
            begin = starts[q] + (MARGIN - ABOVE)
            for h in range(2):
                blocks[q, h * ext : (h + 1) * ext] = strip[h, pl.ds(begin, ext)]
        pick = pl.ds(g * per_copy, per_copy)
        outs.append(pltpu.make_async_copy(blocks.at[pick], out_ref.at[pick], out_sem.at[g]))
        outs[-1].start()
    for copy in outs:
        copy.wait()


def unpack_kernel(capacity, ext, rows_ref, block_ref, out_ref, strip, starts, sem):
    band_rows = out_ref.shape[1]
    facets = block_ref.shape[0]
    end = MARGIN + band_rows
    facet_starts(rows_ref, starts, facets)
    for h in range(2):
        strip[h, 0 : 2 * MARGIN] = jnp.zeros((2 * MARGIN, LANES), jnp.float32)

    copies = []

    def send(begin, stop):
        for h in range(2):
            copies.append(
                pltpu.make_async_copy(
                    strip.at[h, pl.ds(MARGIN + begin, stop - begin)],
                    out_ref.at[0, pl.ds(begin, stop - begin), pl.ds(h * LANES, LANES)],
                    sem.at[len(copies)],
                )
            )
            copies[-1].start()

    shared = lax.broadcasted_iota(jnp.int32, (8, LANES), 0) < 3
    sent = 8
    early = (facets // 2, 3 * facets // 4, 7 * facets // 8, 15 * facets // 16)
    for q in range(facets):
        if q in early:
            ready = (band_rows - (facets - q) * capacity) // 8 * 8 - 8
            send(sent, ready)
            sent = ready
        begin = starts[q] + (MARGIN - ABOVE)
        for h in range(2):
            before = strip[h, pl.ds(begin, 8)]
            strip[h, pl.ds(begin, 8)] = block_ref[q, h * ext : h * ext + 8] + jnp.where(shared, before, 0.0)
            strip[h, pl.ds(begin + 8, ext - 8)] = block_ref[q, h * ext + 8 : (h + 1) * ext]
    for h in range(2):
        strip[h, end - ABOVE : end] += strip[h, MARGIN - ABOVE : MARGIN]
        strip[h, MARGIN : MARGIN + 1] += strip[h, end : end + 1]
    send(0, 8)
    send(sent, band_rows)
    for copy in copies:
        copy.wait()


def stage_kernel(received_ref, dual_hbm, fwd_any, adj_any, first_ref, fwd_ref, adj_ref, sem):
    pairs = ((dual_hbm.at[pl.ds(0, 2)], first_ref), (fwd_any, fwd_ref), (adj_any, adj_ref))
    copies = [pltpu.make_async_copy(src, dst, sem.at[i]) for i, (src, dst) in enumerate(pairs)]
    for copy in copies:
        copy.start()
    for copy in copies:
        copy.wait()


def tail_kernel(tail_ref, begun_hbm, next_hbm, done_ref, sem):
    pair = tail_ref.shape[0]
    copy = pltpu.make_async_copy(tail_ref, next_hbm.at[pl.ds(next_hbm.shape[0] - pair, pair)], sem)
    copy.start()
    done_ref[...] = jnp.zeros_like(done_ref)
    copy.wait()


def facet_kernel(group, ext, taps_ref, thr_ref, info_ref, edge_ref, received_ref, first_ref, dual_hbm, fwd_ref, adj_ref,
                 next_hbm, tail_ref, merged_ref, spill_ref, x_ref,
                 in_slots, out_slots, u_ref, sq_ref, z_ref, in_sem, out_sem):
    steps = dual_hbm.shape[0] // 2
    channels, capacity, columns = dual_hbm.shape[1:]
    rows = group * capacity
    length, below, above = info_ref[0], info_ref[1], info_ref[2]
    inside = info_ref[3].astype(jnp.float32)
    spans = [(1, 3) if step < steps // 2 else (0, TAPS) for step in range(steps)]
    sources = [first_ref] + [in_slots.at[step % 2] for step in range(1, steps)]
    targets = [out_slots.at[step % 2] for step in range(steps - 1)] + [tail_ref]
    fetches = [
        pltpu.make_async_copy(dual_hbm.at[pl.ds(2 * step, 2)], in_slots.at[step % 2], in_sem.at[step % 2])
        for step in range(steps)
    ]
    stores = [
        pltpu.make_async_copy(out_slots.at[step % 2], next_hbm.at[pl.ds(2 * step, 2)], out_sem.at[step % 2])
        for step in range(steps)
    ]
    for step in range(1, 3):
        fetches[step].start()
    z_ref[...] = jnp.zeros_like(z_ref)

    @pl.when(above == 1)
    def _():
        for h in range(2):
            x_ref[:, h * ext : h * ext + ABOVE, :] = inside * edge_ref[:, ABOVE * h : ABOVE * (h + 1), :]

    @pl.when(below == 1)
    def _():
        for h in range(2):
            row = pl.ds(h * ext + ABOVE + length, 1)
            x_ref[:, row, :] = inside * edge_ref[:, ABOVE * h : ABOVE * h + 1, :]

    def analyse(step, i):
        pick = pl.ds(i * group, group)
        begin, stop = spans[step]
        taps = [taps_ref[step * TAPS + k] for k in range(TAPS)]
        halves = []
        for h in range(2):
            total = taps[begin] * x_ref[pick, h * ext + begin : h * ext + begin + capacity, :]
            for k in range(begin + 1, stop):
                total = total + taps[k] * x_ref[pick, h * ext + k : h * ext + k + capacity, :]
            halves.append(total.reshape(rows, LANES))
        filtered = jnp.concatenate(halves, axis=1)
        high = filtered.astype(jnp.bfloat16)
        low = (filtered - high.astype(jnp.float32)).astype(jnp.bfloat16)
        coefficient = jnp.dot(
            jnp.concatenate([high, low], axis=1), fwd_ref[step // 2], preferred_element_type=jnp.float32
        )
        for b in range(2):
            part = coefficient[:, b * columns : (b + 1) * columns].reshape(group, capacity, columns)
            combined = part + sources[step][b, pick].astype(jnp.float32)
            u_ref[step % 2, b, pick] = combined
            sq_ref[step % 2, b] += jnp.sum(combined * combined, axis=0)

    def synthesise(step, i):
        pick = pl.ds(i * group, group)
        begin, stop = spans[step]
        taps = [taps_ref[step * TAPS + k] for k in range(TAPS)]
        parts = []
        for b in range(2):
            scaled = u_ref[step % 2, b, pick] * sq_ref[step % 2, b][None]
            targets[step][b, pick] = scaled.astype(jnp.bfloat16)
            parts.append(scaled.reshape(rows, columns).astype(jnp.bfloat16))
        z = jnp.dot(jnp.concatenate(parts, axis=1), adj_ref[step // 2], preferred_element_type=jnp.float32)
        z = z.reshape(group, capacity, columns)
        for h in range(2):
            z_ref[h, :, 8 : 8 + capacity, :] = z[:, :, h * LANES : (h + 1) * LANES]
        for h in range(2):
            total = taps[begin] * z_ref[h, :, 8 - begin : 8 - begin + ext, :]
            for k in range(begin + 1, stop):
                total = total + taps[k] * z_ref[h, :, 8 - k : 8 - k + ext, :]
            if step == 0:
                merged_ref[pick, h * ext : (h + 1) * ext, :] = total
            else:
                merged_ref[pick, h * ext : (h + 1) * ext, :] += total

    keep = lax.broadcasted_iota(jnp.int32, (capacity, columns), 0) < length
    for stage in range(steps + 1):
        if 0 < stage < steps:
            fetches[stage].wait()
        if stage == 3:
            stores[0].wait()
        if stage < steps:
            sq_ref[stage % 2] = jnp.zeros_like(sq_ref[stage % 2])

        def work(i):
            if stage > 0:
                synthesise(stage - 1, i)
            if stage < steps:
                analyse(stage, i)

        pl.loop(0, channels // group)(work)
        if stage == 1:
            fetches[3].start()
        if 0 < stage < steps:
            stores[stage - 1].start()
        if stage < steps:
            for b in range(2):
                radius = thr_ref[stage * 2 + b]
                scale = radius / jnp.maximum(jnp.sqrt(sq_ref[stage % 2, b]), radius)
                sq_ref[stage % 2, b] = jnp.where(keep, scale, 0.0)

    spill_ref[...] = jnp.zeros_like(spill_ref)

    @pl.when(above == 1)
    def _():
        for h in range(2):
            spill_ref[:, ABOVE * h : ABOVE * (h + 1), :] = merged_ref[:, h * ext : h * ext + ABOVE, :]

    @pl.when(below == 1)
    def _():
        for h in range(2):
            row = pl.ds(h * ext + ABOVE + length, 1)
            spill_ref[:, ABOVE * h : ABOVE * h + 1, :] = merged_ref[:, row, :]

    stores[1].wait()
    stores[2].wait()


def border_kernel(ext, info_ref, sent_ref, spill_ref, stored_ref, merged_ref):
    length, below, above = info_ref[0], info_ref[1], info_ref[2]
    inside = info_ref[4].astype(jnp.float32)

    @pl.when(above == 1)
    def _():
        for h in range(2):
            merged_ref[:, h * ext : h * ext + ABOVE, :] = inside * spill_ref[:, ABOVE * h : ABOVE * (h + 1), :]

    @pl.when(below == 1)
    def _():
        for h in range(2):
            row = pl.ds(h * ext + ABOVE + length, 1)
            merged_ref[:, row, :] = inside * spill_ref[:, ABOVE * h : ABOVE * h + 1, :]


def on_device(image_cube, dual, lowpass, thresholds, facet_rows):
    band = lax.axis_index("grp")
    facet = lax.axis_index("fac")
    facets = lax.axis_size("fac")
    bands = lax.axis_size("grp")
    _, band_rows, columns = image_cube.shape
    subbands, channels, capacity, _ = dual.shape
    ext = capacity + TAPS
    per_step = 4
    strip_rows = MARGIN + band_rows + capacity
    lengths = lax.dynamic_index_in_dim(facet_rows, band, 0, keepdims=False)
    own_length = lax.dynamic_slice_in_dim(lengths, facet, 1)

    row_scratch = [
        pltpu.VMEM((2, strip_rows, LANES), jnp.float32),
        pltpu.SMEM((facets,), jnp.int32),
    ]
    smem = pl.BlockSpec(memory_space=pltpu.SMEM)
    vmem = pl.BlockSpec(memory_space=pltpu.VMEM)
    hbm = pl.BlockSpec(memory_space=pltpu.HBM)
    packed = pl.pallas_call(
        functools.partial(pack_kernel, per_step, ext),
        out_shape=pltpu.HBM((facets, 2 * ext, LANES), jnp.float32),
        in_specs=[hbm, hbm],
        out_specs=hbm,
        scratch_shapes=row_scratch[:2] + [
            pltpu.SMEM(facet_rows.shape, jnp.int32),
            pltpu.VMEM((facets, 2 * ext, LANES), jnp.float32),
            pltpu.SemaphoreType.DMA((2 * (facets // per_step) + 1,)),
            pltpu.SemaphoreType.DMA((facets // per_step,)),
        ],
        compiler_params=pltpu.CompilerParams(vmem_limit_bytes=16 << 20),
        name="pack_facets",
    )(*(pltpu.with_memory_space_constraint(a, pltpu.HBM) for a in (facet_rows, image_cube)))

    received = lax.all_to_all(packed, "fac", split_axis=0, concat_axis=0, tiled=True)

    taps = filter_taps(lowpass)
    matrices = column_matrices(taps, columns)
    forward = jnp.concatenate([matrices[:, 0], matrices[:, 1]], axis=2)
    forward = jnp.concatenate([forward, forward], axis=1)
    swapped = jnp.swapaxes(matrices, 2, 3)
    adjoint = jnp.concatenate([swapped[:, 0], swapped[:, 1]], axis=1)
    group = 16
    dual = pltpu.with_memory_space_constraint(dual, pltpu.HBM)
    pair = (2,) + dual.shape[1:]
    any_space = pl.BlockSpec(memory_space=pl.ANY)
    first, forward, adjoint = pl.pallas_call(
        stage_kernel,
        out_shape=[
            jax.ShapeDtypeStruct(shape, jnp.bfloat16) for shape in (pair, forward.shape, adjoint.shape)
        ],
        in_specs=[any_space, hbm, any_space, any_space],
        out_specs=[vmem] * 3,
        scratch_shapes=[pltpu.SemaphoreType.DMA((3,))],
        compiler_params=pltpu.CompilerParams(vmem_limit_bytes=16 << 20),
        name="stage_first_pair",
    )(received, dual, forward, adjoint)
    below = facet == facets - 1
    above = facet == 0
    before = jnp.where(above, band > 0, band < bands - 1)
    after = jnp.where(above, band < bands - 1, band > 0)
    flags = [flag.astype(jnp.int32) for flag in (below, above, before, after)]
    info = jnp.stack([own_length[0]] + flags)
    edge_row = jnp.where(above, 0, own_length[0] + ABOVE)
    edges = [lax.dynamic_slice_in_dim(received, h * ext + edge_row, ABOVE, 1) for h in range(2)]
    edges = border_shift(jnp.concatenate(edges, axis=1), bands, facets, 1)
    dual_next, tail, merged, spill, _ = pl.pallas_call(
        functools.partial(facet_kernel, group, ext),
        out_shape=(
            pltpu.HBM(dual.shape, jnp.bfloat16),
            jax.ShapeDtypeStruct(pair, jnp.bfloat16),
            jax.ShapeDtypeStruct(received.shape, jnp.float32),
            jax.ShapeDtypeStruct(edges.shape, jnp.float32),
            jax.ShapeDtypeStruct(received.shape, jnp.float32),
        ),
        in_specs=[smem, smem, smem, vmem, vmem, vmem, hbm, vmem, vmem],
        out_specs=(hbm, vmem, vmem, vmem, vmem),
        input_output_aliases={4: 4},
        scratch_shapes=[
            pltpu.VMEM((2,) + pair, jnp.bfloat16),
            pltpu.VMEM((2,) + pair, jnp.bfloat16),
            pltpu.VMEM((2, 2, channels, capacity, columns), jnp.float32),
            pltpu.VMEM((2, 2, capacity, columns), jnp.float32),
            pltpu.VMEM((2, group, capacity + 16, LANES), jnp.float32),
            pltpu.SemaphoreType.DMA((2,)),
            pltpu.SemaphoreType.DMA((2,)),
        ],
        compiler_params=pltpu.CompilerParams(vmem_limit_bytes=36 << 20),
        name="facet_update",
    )(taps.reshape(-1), thresholds, info, edges, received, first, dual, forward, adjoint)

    spill = border_shift(spill, bands, facets, -1)
    dual_next, stored = pl.pallas_call(
        tail_kernel,
        out_shape=(pltpu.HBM(dual.shape, jnp.bfloat16), jax.ShapeDtypeStruct((8, LANES), jnp.float32)),
        in_specs=[vmem, hbm],
        out_specs=(hbm, vmem),
        input_output_aliases={1: 0},
        scratch_shapes=[pltpu.SemaphoreType.DMA],
        compiler_params=pltpu.CompilerParams(vmem_limit_bytes=16 << 20),
        name="store_last_pair",
    )(tail, dual_next)
    merged = pl.pallas_call(
        functools.partial(border_kernel, ext),
        out_shape=jax.ShapeDtypeStruct(received.shape, jnp.float32),
        in_specs=[smem, vmem, vmem, vmem],
        out_specs=vmem,
        input_output_aliases={1: 0},
        compiler_params=pltpu.CompilerParams(vmem_limit_bytes=16 << 20),
        name="add_border_rows",
    )(info, merged, spill, stored)
    returned = lax.all_to_all(merged, "fac", split_axis=0, concat_axis=0, tiled=True)

    prior_term = pl.pallas_call(
        functools.partial(unpack_kernel, capacity, ext),
        out_shape=jax.ShapeDtypeStruct(image_cube.shape, jnp.float32),
        in_specs=[smem, vmem],
        out_specs=hbm,
        scratch_shapes=row_scratch[:2] + [pltpu.SemaphoreType.DMA((12,))],
        compiler_params=pltpu.CompilerParams(vmem_limit_bytes=16 << 20),
        name="unpack_facets",
    )(facet_rows, returned)
    return dual_next, prior_term


def solution(mesh):
    placed = (P("fac", "grp", None), P(None, None, ("grp", "fac"), None), P(), P(), P())
    return jax.shard_map(
        on_device,
        mesh=mesh,
        in_specs=placed,
        out_specs=(P(None, None, ("grp", "fac"), None), P("fac", "grp", None)),
        check_vma=False,
    )
```
